512 devices in a mesh: layer: 8 (over x, z_hi), ex: 16 (over y, core), width: 4 (over z_lo).
Axes of the slice: x: 4, y: 8, z: 8 (z_hi: 2, z_lo: 4; z = z_hi * 4 + z_lo), core: 2. Of those that a mesh axis runs over, the one named last changes fastest.
Arguments:
- activations: bfloat16 [8, 128, 32, 8192], P('layer', 'ex', None, 'width'), may hold values from -6 to 6
- gradients: bfloat16 [8, 128, 32, 28672], P('layer', 'ex', None, 'width'), may hold values from -6 to 6
- act_scale: float32 [8, 8192], P('layer', 'width'), may hold values from 0.25 to 4
- grad_scale: float32 [8, 28672], P('layer', 'width'), may hold values from 0.25 to 4
- counts: int32 [128], P('ex'), may hold values from 1 to 32, 3072 in all
- loss_mask: int32 [128, 32], P('ex'), may hold values 0 or 1
Outputs:
- influence: float32 [3, 128, 8], P(None, 'ex', 'layer')
The draws below stay inside these ranges and needn't reach their ends.
Inputs may be any that keep to these rules, and one draw needn't show every extreme that they name: counts[e] is the number of filled token slots of example e; the largest is reached in every draw.
All inputs are finite; a program needn't handle non-finite values. No bound on the sum of `counts` or of `loss_mask` on one device may be relied on, other than what follows from the above.
Results may differ from the reference program's by a relative error of at most 0.004.
Values may be sent and summed in bfloat16 or wider, within the bound.
No kernel may reach another device: no remote copies, remote signals or barrier semaphores. Data moves between devices by JAX's collectives and lax.ppermute only.
A program may use at most 64 MiB of HBM per device.

```python
import math
import jax
import jax.numpy as jnp
import numpy as np
from jax import lax

D = 8192
FF = 28672
EX_DEV = 8
TOK = 32
HOPS = 2
LAYERS = 8
EXAMPLES = 128


def set_ends(drawn, stream_key, smallest, high):
    dims = drawn.shape
    spot = [jax.random.randint(jax.random.fold_in(stream_key, axis), (), 0, dims[axis]) for axis in range(len(dims))]
    drawn = drawn.at[tuple(spot)].set(smallest)
    longest = dims.index(max(dims))
    spot[longest] = (spot[longest] + 1) % dims[longest]
    return drawn.at[tuple(spot)].set(high)


def steps_of(rng, extent, cuts, low, high):
    level, own = 1.0, jax.random.fold_in(rng, 6)
    for position, parts in cuts:
        draws = jnp.exp(jax.random.uniform(jax.random.fold_in(own, position), (parts,), jnp.float32, low / len(cuts), high / len(cuts)))
        level = level * jnp.repeat(draws, extent[position] // parts).reshape([-1 if axis == position else 1 for axis in range(len(extent))])
    return level


def length_profile(count, total, bound, slope):
    loads = [(1 << 20) // math.isqrt(rank ** slope) + 1 for rank in range(2, count + 1)]
    rest, given = total - bound - (count - 1), [1] * (count - 1)
    while rest > 0:
        candidates = [i for i in range(count - 1) if given[i] < bound]
        pool, left = sum([loads[i] for i in candidates]), rest
        for i in candidates:
            addition = min(bound - given[i], max(1, left * loads[i] // pool), rest)
            given[i] = given[i] + addition
            rest = rest - addition
    return np.array([bound] + given)


def uneven_parts(own_key, amount, total, most, lean):
    if amount == 2:
        one = jax.random.randint(own_key, (), max(1, total - most), min(most, total - 1) + 1)
        return jnp.stack([one, total - one])
    sizes = jnp.asarray(length_profile(amount, total, most, lean), jnp.int32)
    pairs = (amount - 1) // 2
    giver, receiver = sizes[1:1 + 2 * pairs:2], sizes[2:2 + 2 * pairs:2]
    slack = jnp.minimum(giver - 1, most - receiver)
    moved = jax.random.randint(jax.random.fold_in(own_key, 1), (pairs,), 0, 1 << 20) % (slack + 1)
    sizes = sizes.at[1:1 + 2 * pairs:2].set(giver - moved).at[2:2 + 2 * pairs:2].set(receiver + moved)
    return sizes[jax.random.permutation(jax.random.fold_in(own_key, 2), amount)]


def bell_draw(rng, shape, deviation, bound, pieces=(), kind=jnp.bfloat16):
    gain = steps_of(rng, shape, pieces, -0.22, 0.18) if pieces else 1.0
    drawn = jax.random.normal(rng, shape, jnp.float32) * deviation * gain
    return jnp.minimum(jnp.maximum(drawn, -bound), bound).astype(kind)


def setup_inputs(seed: int = 0) -> dict:
    keys = jax.random.split(jax.random.key(seed), 7)
    return {
        "activations": bell_draw(keys[0], (LAYERS, EXAMPLES, TOK, D), 1.0, 6.0, ((0, 8), (1, 16), (3, 4))),
        "gradients": bell_draw(keys[1], (LAYERS, EXAMPLES, TOK, FF), 1.0, 6.0, ((0, 8), (1, 16), (3, 4))),
        "act_scale": jnp.clip(jnp.exp(math.log(4.0) - 2.7725887 * jax.random.uniform(keys[2], (LAYERS, D), jnp.float32) ** steps_of(keys[2], (LAYERS, D), ((0, 8), (1, 4)), -0.2, 0.2)), 0.25, 4.0),
        "grad_scale": jnp.clip(jnp.exp(math.log(4.0) - 2.7725887 * jax.random.uniform(keys[3], (LAYERS, FF), jnp.float32) ** steps_of(keys[3], (LAYERS, FF), ((0, 8), (1, 4)), -0.2, 0.2)), 0.25, 4.0),
        "counts": uneven_parts(keys[4], EXAMPLES, EXAMPLES * TOK * 3 // 4, TOK, 0).astype(jnp.int32),
        "loss_mask": set_ends((jax.random.randint(keys[5], (EXAMPLES, TOK), 0, 4) < 3).astype(jnp.int32), jax.random.fold_in(keys[5], 1), 0, 1),
    }


def reference(activations, gradients, act_scale, grad_scale, counts, loss_mask):
    ex_count = activations.shape[1]
    blocks = ex_count // EX_DEV
    row_count = EX_DEV * TOK
    positions = jnp.arange(TOK, dtype=jnp.int32)
    token_weight = (positions[None, :] < counts[:, None]).astype(jnp.int32) * loss_mask
    weight_rows = token_weight.astype(jnp.float32).reshape(blocks, row_count)
    factor = 1.0 / (math.sqrt(D * FF) * TOK)

    def layer_term(running, layer_data):
        layer_acts, layer_grads, gain_acts, gain_grads = layer_data
        stat_acts = (layer_acts.astype(jnp.float32) * gain_acts).astype(jnp.bfloat16).reshape(blocks, row_count, -1)
        stat_grads = (layer_grads.astype(jnp.float32) * gain_grads).astype(jnp.bfloat16).reshape(blocks, row_count, -1)
        move_acts = layer_acts.reshape(blocks, row_count, -1)
        move_grads = layer_grads.reshape(blocks, row_count, -1)
        per_hop = []
        for distance in range(HOPS + 1):

            def one_block(anchor):
                partner = (anchor - distance) % blocks
                act_gram = jnp.dot(stat_acts[anchor], move_acts[partner].T, preferred_element_type=jnp.float32)
                grad_gram = jnp.dot(stat_grads[anchor], move_grads[partner].T, preferred_element_type=jnp.float32)
                product = act_gram * grad_gram * weight_rows[anchor][:, None] * weight_rows[partner][None, :]
                return product.reshape(EX_DEV, TOK, EX_DEV, TOK).sum(axis=(1, 3))
            scores = lax.map(one_block, jnp.arange(blocks, dtype=jnp.int32))
            per_hop.append(scores.reshape(ex_count, EX_DEV))
        return (running + jnp.stack(per_hop) * factor, None)
    start = jnp.zeros((HOPS + 1, ex_count, EX_DEV), jnp.float32)
    influence_sum, _ = lax.scan(layer_term, start, (activations, gradients, act_scale, grad_scale))
    not_self = (jnp.arange(ex_count, dtype=jnp.int32)[:, None] % EX_DEV != jnp.arange(EX_DEV, dtype=jnp.int32)[None, :]).astype(jnp.float32)
    first = influence_sum[0] * not_self
    return jnp.concatenate([first[None], influence_sum[1:]], axis=0)
```

```python
import functools
import math

import jax
import jax.numpy as jnp
from jax import lax
from jax.experimental import pallas as pl
from jax.experimental.pallas import tpu as pltpu
from jax.sharding import PartitionSpec as P

D = 8192
FF = 28672
HOPS = 2
CAP = 176
TALL = 192
OWN = 384
WIDE = 640
TAG = 128
PACK_TILE = 1792
BF16 = jnp.bfloat16
F32 = jnp.float32
VMEM_LIMIT = 48 * 1024 * 1024


def from_behind(value, axis, steps):
    count = lax.axis_size(axis)
    pairs = [(source, (source + steps) % count) for source in range(count)]
    return lax.ppermute(value, axis, pairs)


def plain(activations, gradients, act_scale, grad_scale, weight_rows, tok_slots):
    row_count = weight_rows.shape[0]
    ex_local = row_count // tok_slots
    own_acts = activations[0].reshape(row_count, -1)
    own_grads = gradients[0].reshape(row_count, -1)
    stat_acts = (own_acts.astype(F32) * act_scale[0]).astype(BF16)
    stat_grads = (own_grads.astype(F32) * grad_scale[0]).astype(BF16)
    factor = 1.0 / (math.sqrt(D * FF) * tok_slots)
    contract = (((1,), (1,)), ((), ()))

    def pair_scores(partner):
        move_acts, move_grads, move_weight = partner
        act_gram = lax.dot_general(stat_acts, move_acts, contract, preferred_element_type=F32)
        grad_gram = lax.dot_general(stat_grads, move_grads, contract, preferred_element_type=F32)
        act_gram, grad_gram = lax.psum((act_gram, grad_gram), "width")
        product = act_gram * grad_gram * weight_rows[:, None] * move_weight.astype(F32)[None, :]
        return product.reshape(ex_local, tok_slots, ex_local, tok_slots).sum(axis=(1, 3)) * factor

    partner = (own_acts, own_grads, weight_rows.astype(BF16))
    scores = [pair_scores(partner)]
    for distance in range(HOPS):
        partner = tuple(from_behind(value, "ex", 1) for value in partner)
        scores.append(pair_scores(partner))
    local_ex = lax.broadcasted_iota(jnp.int32, (ex_local, ex_local), 0)
    column_ex = lax.broadcasted_iota(jnp.int32, (ex_local, ex_local), 1)
    scores[0] = scores[0] * (local_ex != column_ex).astype(F32)
    return lax.psum_scatter(jnp.stack(scores), "layer", scatter_dimension=2, tiled=True)


def token_weights(counts_ref, mask_ref):
    ex_local, tok_slots = mask_ref.shape
    rows = ex_local * tok_slots
    position = lax.broadcasted_iota(jnp.int32, (ex_local, tok_slots), 1)
    example = lax.broadcasted_iota(jnp.int32, (ex_local, tok_slots), 0)
    filled = jnp.zeros((ex_local, tok_slots), jnp.int32)
    for place in range(ex_local):
        filled = jnp.where(example == place, counts_ref[place], filled)
    weight = jnp.where((position < filled) & (mask_ref[...] == 1), 1.0, 0.0)
    lane = lax.broadcasted_iota(jnp.int32, (tok_slots, rows), 1)
    slot = lax.broadcasted_iota(jnp.int32, (tok_slots, rows), 0)
    spread = jnp.where(lane % tok_slots == slot, 1.0, 0.0).astype(BF16)
    wide = jnp.dot(weight.astype(BF16), spread, preferred_element_type=F32)
    owner = lax.broadcasted_iota(jnp.int32, (ex_local, rows), 1) // tok_slots
    row = lax.broadcasted_iota(jnp.int32, (ex_local, rows), 0)
    return jnp.sum(jnp.where(owner == row, wide, 0.0), axis=0, keepdims=True)


def pack_acts_kernel(counts_ref, mask_ref, rows_ref, packed_ref, pick_ref, over_ref):
    features, rows = rows_ref.shape[1], rows_ref.shape[0]
    tok_slots = mask_ref.shape[1]
    weights = token_weights(counts_ref, mask_ref)
    before = lax.broadcasted_iota(jnp.int32, (rows, rows), 0)
    upto = lax.broadcasted_iota(jnp.int32, (rows, rows), 1)
    ramp = jnp.where(before <= upto, 1.0, 0.0).astype(BF16)
    lifted = jnp.broadcast_to(weights, (16, rows)).astype(BF16)
    rank = jnp.dot(lifted, ramp, preferred_element_type=F32)[0:1]
    slot = lax.broadcasted_iota(jnp.int32, (CAP, rows), 0).astype(F32) + 1.0
    pick = (jnp.where(slot == rank, 1.0, 0.0) * weights).astype(BF16)
    pick_ref[...] = pick
    total = jnp.broadcast_to(jnp.sum(weights, axis=1, keepdims=True), over_ref.shape)
    over_ref[...] = jnp.where(total > CAP, 1.0, 0.0)
    packed_ref[:, :features] = jnp.dot(pick, rows_ref[...], preferred_element_type=F32).astype(BF16)
    shape = (rows, TAG)
    example = lax.broadcasted_iota(jnp.int32, shape, 0) // tok_slots
    lane = lax.broadcasted_iota(jnp.int32, shape, 1)
    short = jnp.where(lane % 8 == example, 1.0, 0.0)
    long = jnp.where((lane % 32) // 4 == example, 1.0, 0.0)
    tags = jnp.where(lane < 32, short, long).astype(BF16)
    packed_ref[:, features:] = jnp.dot(pick, tags, preferred_element_type=F32).astype(BF16)


def pack_acts(counts, mask, rows):
    count, features = rows.shape
    vmem = pl.BlockSpec(memory_space=pltpu.VMEM)
    return pl.pallas_call(
        pack_acts_kernel,
        in_specs=[pl.BlockSpec(memory_space=pltpu.SMEM), vmem, vmem],
        out_specs=[vmem, vmem, vmem],
        out_shape=[
            jax.ShapeDtypeStruct((CAP, features + TAG), BF16),
            jax.ShapeDtypeStruct((CAP, count), BF16),
            jax.ShapeDtypeStruct((16, TAG), F32),
        ],
        compiler_params=pltpu.CompilerParams(vmem_limit_bytes=VMEM_LIMIT),
        cost_estimate=pl.CostEstimate(
            flops=2 * CAP * count * features, bytes_accessed=4 * count * features, transcendentals=0
        ),
        name="pack_acts",
    )(counts, mask, rows)


def pack_grads_kernel(pick_ref, rows_ref, after_ref, packed_ref):
    del after_ref
    packed_ref[...] = jnp.dot(pick_ref[...], rows_ref[...], preferred_element_type=F32).astype(BF16)


def pack_grads(pick, rows, after, tile=PACK_TILE):
    count, features = rows.shape
    return pl.pallas_call(
        pack_grads_kernel,
        grid=(features // tile,),
        in_specs=[
            pl.BlockSpec((CAP, count), lambda step: (0, 0)),
            pl.BlockSpec((count, tile), lambda step: (0, step)),
            pl.BlockSpec(memory_space=pl.ANY),
        ],
        out_specs=pl.BlockSpec((CAP, tile), lambda step: (0, step)),
        out_shape=jax.ShapeDtypeStruct((CAP, features), BF16),
        compiler_params=pltpu.CompilerParams(vmem_limit_bytes=VMEM_LIMIT),
        cost_estimate=pl.CostEstimate(
            flops=40 * CAP * count * features, bytes_accessed=4 * count * features, transcendentals=0
        ),
        name="pack_grads",
    )(pick, rows, after)


def add_grams(parity, own_ref, near_ref, far_ref, scale_ref, gram_ref):
    contract = (((1,), (1,)), ((), ()))

    def scaled(ref):
        return (ref[...].astype(F32) * scale_ref[...]).astype(BF16)

    def pairs(left_ref, last_ref):
        right = jnp.concatenate([near_ref[...], last_ref[...]], axis=0)
        gram_ref[:CAP, : 2 * CAP] += lax.dot_general(
            scaled(left_ref), right, contract, preferred_element_type=F32
        )

    gram_ref[:CAP, OWN : OWN + CAP] += lax.dot_general(
        scaled(own_ref), own_ref[...], contract, preferred_element_type=F32
    )

    @pl.when(parity == 1)
    def _():
        pairs(own_ref, far_ref)

    @pl.when(parity == 0)
    def _():
        pairs(far_ref, own_ref)


def gram_kernel(own_ref, near_ref, far_ref, scale_ref, parity_ref, note_ref, gram_ref, said_ref):
    @pl.when(pl.program_id(0) == 0)
    def _():
        gram_ref[...] = jnp.zeros_like(gram_ref)
        said_ref[...] = jnp.max(note_ref[...], axis=0, keepdims=True)

    add_grams(parity_ref[0], own_ref, near_ref, far_ref, scale_ref, gram_ref)


def gram(own, near, far, scale, parity, note, tile, weight):
    features = scale.shape[1]
    block = pl.BlockSpec((CAP, tile), lambda step: (0, step))
    return pl.pallas_call(
        gram_kernel,
        grid=(features // tile,),
        in_specs=[
            block,
            block,
            block,
            pl.BlockSpec((1, tile), lambda step: (0, step)),
            pl.BlockSpec(memory_space=pltpu.SMEM),
            pl.BlockSpec(note.shape, lambda step: (0, 0)),
        ],
        out_specs=[
            pl.BlockSpec((TALL, WIDE), lambda step: (0, 0)),
            pl.BlockSpec((1, TAG), lambda step: (0, 0)),
        ],
        out_shape=[jax.ShapeDtypeStruct((TALL, WIDE), F32), jax.ShapeDtypeStruct((1, TAG), F32)],
        compiler_params=pltpu.CompilerParams(vmem_limit_bytes=VMEM_LIMIT),
        cost_estimate=pl.CostEstimate(
            flops=weight * 6 * 256 * 256 * features, bytes_accessed=6 * CAP * features, transcendentals=0
        ),
        name="gram",
    )(own, near, far, scale, parity, note)


def spread_kernel(parts_ref, out_ref):
    total = parts_ref[0]
    for part in range(1, parts_ref.shape[0]):
        total = total + parts_ref[part]
    for part in range(out_ref.shape[0]):
        out_ref[part] = total


def sum_and_spread(parts):
    return pl.pallas_call(
        spread_kernel,
        out_shape=jax.ShapeDtypeStruct(parts.shape, F32),
        compiler_params=pltpu.CompilerParams(vmem_limit_bytes=VMEM_LIMIT),
        name="sum_and_spread",
    )(parts)


def exact_dot(left, one_hot, contract):
    total = None
    for _ in range(3):
        part = left.astype(BF16)
        left = left - part.astype(F32)
        term = lax.dot_general(part, one_hot, contract, preferred_element_type=F32)
        total = term if total is None else total + term
    return total


def finish_kernel(
    factor, grad_ref, act_ref, parity_ref, own_tag_ref, near_tag_ref, far_tag_ref, out_ref, tag_ref
):
    product = grad_ref[...] * act_ref[...]
    lane = lax.broadcasted_iota(jnp.int32, (CAP, TAG), 1) // 32
    odd = (parity_ref[0] == 1).astype(F32)
    own, near, far = (ref[...].astype(F32) for ref in (own_tag_ref, near_tag_ref, far_tag_ref))
    last = odd * far + (1.0 - odd) * own
    left = odd * own + (1.0 - odd) * far
    tag_ref[...] = jnp.zeros_like(tag_ref)
    tag_ref[:CAP] = jnp.where(lane == 1, near, 0.0).astype(BF16)
    tag_ref[CAP : 2 * CAP] = jnp.where(lane == 2, last, 0.0).astype(BF16)
    tag_ref[OWN : OWN + CAP] = jnp.where(lane == 3, own, 0.0).astype(BF16)
    by_column = exact_dot(product, tag_ref[...], (((1,), (0,)), ((), ())))[:CAP]
    by_row = (((0,), (0,)), ((), ()))
    pairs = exact_dot(by_column, left.astype(BF16), by_row)
    selves = exact_dot(by_column, own.astype(BF16), by_row)
    shape = (32, TAG)
    column = lax.broadcasted_iota(jnp.int32, shape, 0) // 4
    place = lax.broadcasted_iota(jnp.int32, shape, 1)
    out_ref[...] = factor * (
        jnp.where((place < 8) & (place != column), selves[96:128], 0.0)
        + jnp.where((place >= 8) & (place < 16), pairs[32:64], 0.0)
        + jnp.where((place >= 16) & (place < 24), pairs[64:96], 0.0)
    )


def finish(factor, grad_gram, act_gram, parity, tags):
    tag_at = tags[0].shape[1] // TAG - 1
    whole = pl.BlockSpec((TALL, WIDE), lambda step: (0, 0))
    tag = pl.BlockSpec((CAP, TAG), lambda step: (0, tag_at))
    return pl.pallas_call(
        functools.partial(finish_kernel, factor),
        grid=(1,),
        in_specs=[whole, whole, pl.BlockSpec(memory_space=pltpu.SMEM), tag, tag, tag],
        out_specs=pl.BlockSpec((32, TAG), lambda step: (0, 0)),
        out_shape=jax.ShapeDtypeStruct((32, TAG), F32),
        scratch_shapes=[pltpu.VMEM((WIDE, TAG), BF16)],
        compiler_params=pltpu.CompilerParams(vmem_limit_bytes=VMEM_LIMIT),
        name="finish",
    )(grad_gram, act_gram, parity, *tags)


def far_swap(value):
    count = lax.axis_size("ex")
    pairs = [(e, (e + (2 if e % 2 else -2)) % count) for e in range(count)]
    return lax.ppermute(value, "ex", pairs)


def near_swap(value):
    count = lax.axis_size("ex")
    return lax.ppermute(value, "ex", [(e, e ^ 1) for e in range(count)])


def sum_over_width(value):
    parts = lax.axis_size("width")
    split = value.reshape(parts, TALL // parts, WIDE)
    spread = sum_and_spread(lax.all_to_all(split, "width", 0, 0))
    return lax.all_to_all(spread, "width", 0, 0).reshape(TALL, WIDE)


def local(activations, gradients, act_scale, grad_scale, counts, loss_mask):
    ex_local, tok_slots = loss_mask.shape
    row_count = ex_local * tok_slots
    own_acts = activations[0].reshape(row_count, -1)
    own_grads = gradients[0].reshape(row_count, -1)
    positions = lax.broadcasted_iota(jnp.int32, (ex_local, tok_slots), 1)
    token_weight = (positions < counts[:, None]).astype(jnp.int32) * loss_mask
    weight_rows = token_weight.astype(F32).reshape(row_count)
    parity = (lax.axis_index("ex") % 2).astype(jnp.int32).reshape(1)
    factor = 1.0 / (math.sqrt(D * FF) * tok_slots)

    acts, pick, over = pack_acts(counts, loss_mask, own_acts)
    far_acts, near_acts = far_swap(acts), near_swap(acts)
    grads = pack_grads(pick, own_grads, near_acts)
    far_grads, near_grads = far_swap(grads), near_swap(grads)
    over_all = lax.all_to_all(over, "ex", 0, 0, tiled=True)

    act_gram, _ = gram(acts, near_acts, far_acts, act_scale, parity, over, 1024, 300)
    act_gram = sum_over_width(act_gram)
    grad_gram, most = gram(grads, near_grads, far_grads, grad_scale, parity, over_all, PACK_TILE, 1)
    crowded = most[0, 0] > 0.0
    scores = finish(factor, grad_gram, act_gram, parity, (acts, near_acts, far_acts))
    mine = lax.all_to_all(scores, ("layer", "width"), 0, 0, tiled=True).sum(axis=0)
    ahead = from_behind(mine, "ex", 2)
    place = lax.broadcasted_iota(jnp.int32, mine.shape, 0)
    kept = jnp.where((place < 8) | (parity[0] == 1), mine, ahead)
    quick = kept[: 8 * (HOPS + 1)].reshape(HOPS + 1, ex_local, 1)
    return lax.cond(
        crowded,
        lambda: plain(activations, gradients, act_scale, grad_scale, weight_rows, tok_slots),
        lambda: quick,
    )


def solution(mesh):
    in_specs = (
        P("layer", "ex", None, "width"),
        P("layer", "ex", None, "width"),
        P("layer", "width"),
        P("layer", "width"),
        P("ex"),
        P("ex", None),
    )
    out_specs = P(None, "ex", "layer")
    return jax.shard_map(local, mesh=mesh, in_specs=in_specs, out_specs=out_specs, check_vma=False)
```

```python
import functools
import math

import jax
import jax.numpy as jnp
from jax import lax
from jax.experimental import pallas as pl
from jax.experimental.pallas import tpu as pltpu
from jax.sharding import PartitionSpec as P

D = 8192
FF = 28672
HOPS = 2
CAP = 176
TALL = 192
OWN = 384
WIDE = 640
TAG = 128
TILE = 3584
BF16 = jnp.bfloat16
F32 = jnp.float32
VMEM_LIMIT = 24 * 1024 * 1024


def from_behind(value, axis, steps):
    count = lax.axis_size(axis)
    pairs = [(source, (source + steps) % count) for source in range(count)]
    return lax.ppermute(value, axis, pairs)


def butterfly_sum(value, axis):
    count, step = lax.axis_size(axis), 1
    while step < count:
        value = value + lax.ppermute(value, axis, [(place, place ^ step) for place in range(count)])
        step *= 2
    return value


def plain(activations, gradients, act_scale, grad_scale, weight_rows, tok_slots):
    row_count = weight_rows.shape[0]
    ex_local = row_count // tok_slots
    own_acts = activations[0].reshape(row_count, -1)
    own_grads = gradients[0].reshape(row_count, -1)
    stat_acts = (own_acts.astype(F32) * act_scale[0]).astype(BF16)
    stat_grads = (own_grads.astype(F32) * grad_scale[0]).astype(BF16)
    factor = 1.0 / (math.sqrt(D * FF) * tok_slots)
    contract = (((1,), (1,)), ((), ()))

    def pair_scores(partner):
        move_acts, move_grads, move_weight = partner
        act_gram = lax.dot_general(stat_acts, move_acts, contract, preferred_element_type=F32)
        grad_gram = lax.dot_general(stat_grads, move_grads, contract, preferred_element_type=F32)
        act_gram, grad_gram = butterfly_sum(act_gram, "width"), butterfly_sum(grad_gram, "width")
        product = act_gram * grad_gram * weight_rows[:, None] * move_weight.astype(F32)[None, :]
        return product.reshape(ex_local, tok_slots, ex_local, tok_slots).sum(axis=(1, 3)) * factor

    partner = (own_acts, own_grads, weight_rows.astype(BF16))
    scores = [pair_scores(partner)]
    for distance in range(HOPS):
        partner = tuple(from_behind(value, "ex", 1) for value in partner)
        scores.append(pair_scores(partner))
    local_ex = lax.broadcasted_iota(jnp.int32, (ex_local, ex_local), 0)
    column_ex = lax.broadcasted_iota(jnp.int32, (ex_local, ex_local), 1)
    scores[0] = scores[0] * (local_ex != column_ex).astype(F32)
    summed = butterfly_sum(jnp.stack(scores), "layer")
    column = lax.axis_index("layer") * (ex_local // lax.axis_size("layer"))
    return lax.dynamic_slice_in_dim(summed, column, ex_local // lax.axis_size("layer"), axis=2)


def token_weights(counts_ref, mask_ref):
    ex_local, tok_slots = mask_ref.shape
    rows = ex_local * tok_slots
    position = lax.broadcasted_iota(jnp.int32, (ex_local, tok_slots), 1)
    example = lax.broadcasted_iota(jnp.int32, (ex_local, tok_slots), 0)
    filled = jnp.zeros((ex_local, tok_slots), jnp.int32)
    for place in range(ex_local):
        filled = jnp.where(example == place, counts_ref[place], filled)
    weight = jnp.where((position < filled) & (mask_ref[...] == 1), 1.0, 0.0)
    lane = lax.broadcasted_iota(jnp.int32, (tok_slots, rows), 1)
    slot = lax.broadcasted_iota(jnp.int32, (tok_slots, rows), 0)
    spread = jnp.where(lane % tok_slots == slot, 1.0, 0.0).astype(BF16)
    wide = jnp.dot(weight.astype(BF16), spread, preferred_element_type=F32)
    owner = lax.broadcasted_iota(jnp.int32, (ex_local, rows), 1) // tok_slots
    row = lax.broadcasted_iota(jnp.int32, (ex_local, rows), 0)
    return jnp.sum(jnp.where(owner == row, wide, 0.0), axis=0, keepdims=True)


def pack_acts_kernel(counts_ref, mask_ref, rows_ref, packed_ref, pick_ref, over_ref):
    features, rows = rows_ref.shape[1], rows_ref.shape[0]
    tok_slots = mask_ref.shape[1]
    weights = token_weights(counts_ref, mask_ref)
    before = lax.broadcasted_iota(jnp.int32, (rows, rows), 0)
    upto = lax.broadcasted_iota(jnp.int32, (rows, rows), 1)
    ramp = jnp.where(before <= upto, 1.0, 0.0).astype(BF16)
    lifted = jnp.broadcast_to(weights, (16, rows)).astype(BF16)
    rank = jnp.dot(lifted, ramp, preferred_element_type=F32)[0:1]
    slot = lax.broadcasted_iota(jnp.int32, (CAP, rows), 0).astype(F32) + 1.0
    pick = (jnp.where(slot == rank, 1.0, 0.0) * weights).astype(BF16)
    pick_ref[...] = pick
    total = jnp.broadcast_to(jnp.sum(weights, axis=1, keepdims=True), over_ref.shape)
    over_ref[...] = jnp.where(total > CAP, 1.0, 0.0)
    packed_ref[:, :features] = jnp.dot(pick, rows_ref[...], preferred_element_type=F32).astype(BF16)
    shape = (rows, TAG)
    example = lax.broadcasted_iota(jnp.int32, shape, 0) // tok_slots
    lane = lax.broadcasted_iota(jnp.int32, shape, 1)
    short = jnp.where(lane % 8 == example, 1.0, 0.0)
    long = jnp.where((lane % 32) // 4 == example, 1.0, 0.0)
    tags = jnp.where(lane < 32, short, long).astype(BF16)
    packed_ref[:, features:] = jnp.dot(pick, tags, preferred_element_type=F32).astype(BF16)


def pack_acts(counts, mask, rows):
    count, features = rows.shape
    vmem = pl.BlockSpec(memory_space=pltpu.VMEM)
    return pl.pallas_call(
        pack_acts_kernel,
        grid=(1,),
        in_specs=[
            pl.BlockSpec(memory_space=pltpu.SMEM),
            pl.BlockSpec(mask.shape, lambda step: (0, 0)),
            pl.BlockSpec(rows.shape, lambda step: (0, 0)),
        ],
        out_specs=[vmem, vmem, vmem],
        out_shape=[
            jax.ShapeDtypeStruct((CAP, features + TAG), BF16),
            jax.ShapeDtypeStruct((CAP, count), BF16),
            jax.ShapeDtypeStruct((16, TAG), F32),
        ],
        compiler_params=pltpu.CompilerParams(vmem_limit_bytes=VMEM_LIMIT),
        cost_estimate=pl.CostEstimate(
            flops=2 * CAP * count * features, bytes_accessed=4 * count * features, transcendentals=0
        ),
        name="pack_acts",
    )(counts, mask, rows)


def pack_grads_kernel(pick_ref, rows_ref, after_ref, packed_ref):
    del after_ref
    packed_ref[...] = jnp.dot(pick_ref[...], rows_ref[...], preferred_element_type=F32).astype(BF16)


def pack_grads(pick, rows, after):
    count, features = rows.shape
    return pl.pallas_call(
        pack_grads_kernel,
        grid=(features // TILE,),
        in_specs=[
            pl.BlockSpec((CAP, count), lambda step: (0, 0)),
            pl.BlockSpec((count, TILE), lambda step: (0, step)),
            pl.BlockSpec(memory_space=pl.ANY),
        ],
        out_specs=pl.BlockSpec((CAP, TILE), lambda step: (0, step)),
        out_shape=jax.ShapeDtypeStruct((CAP, features), BF16),
        compiler_params=pltpu.CompilerParams(vmem_limit_bytes=VMEM_LIMIT),
        cost_estimate=pl.CostEstimate(
            flops=40 * CAP * count * features, bytes_accessed=4 * count * features, transcendentals=0
        ),
        name="pack_grads",
    )(pick, rows, after)


def gram_kernel(far_ref, near_ref, own_ref, scale_ref, parity_ref, gram_ref):
    contract = (((1,), (1,)), ((), ()))

    @pl.when(pl.program_id(0) == 0)
    def _():
        gram_ref[...] = jnp.zeros_like(gram_ref)

    def scaled(ref):
        return (ref[...].astype(F32) * scale_ref[...]).astype(BF16)

    def add(columns, left, right):
        gram_ref[:CAP, columns] += lax.dot_general(left, right, contract, preferred_element_type=F32)

    pair, alone = slice(0, 2 * CAP), slice(OWN, OWN + CAP)

    @pl.when(parity_ref[0] == 1)
    def _():
        left = scaled(own_ref)
        add(pair, left, jnp.concatenate([near_ref[...], far_ref[...]], axis=0))
        add(alone, left, own_ref[...])

    @pl.when(parity_ref[0] == 0)
    def _():
        add(pair, scaled(far_ref), jnp.concatenate([near_ref[...], own_ref[...]], axis=0))
        add(alone, scaled(own_ref), own_ref[...])


def gram(own, near, far, scale, parity, weight):
    features = scale.shape[1]
    tile = min(features, TILE)
    block = pl.BlockSpec((CAP, tile), lambda step: (0, step))
    return pl.pallas_call(
        gram_kernel,
        grid=(features // tile,),
        in_specs=[
            block,
            block,
            block,
            pl.BlockSpec((1, tile), lambda step: (0, step)),
            pl.BlockSpec(memory_space=pltpu.SMEM),
        ],
        out_specs=pl.BlockSpec((TALL, WIDE), lambda step: (0, 0)),
        out_shape=jax.ShapeDtypeStruct((TALL, WIDE), F32),
        compiler_params=pltpu.CompilerParams(vmem_limit_bytes=VMEM_LIMIT),
        cost_estimate=pl.CostEstimate(
            flops=weight * 6 * 256 * 256 * features, bytes_accessed=6 * CAP * features, transcendentals=0
        ),
        name="gram",
    )(far, near, own, scale, parity)


def spread_kernel(parts_ref, note_ref, out_ref, said_ref):
    total = parts_ref[0]
    for part in range(1, parts_ref.shape[0]):
        total = total + parts_ref[part]
    rounded = total.astype(BF16)
    for part in range(out_ref.shape[0]):
        out_ref[part] = rounded
    said_ref[...] = jnp.max(note_ref[...], axis=0, keepdims=True)


def sum_and_spread(parts, note):
    return pl.pallas_call(
        spread_kernel,
        out_shape=[
            jax.ShapeDtypeStruct(parts.shape, BF16),
            jax.ShapeDtypeStruct((1, note.shape[1]), F32),
        ],
        compiler_params=pltpu.CompilerParams(vmem_limit_bytes=VMEM_LIMIT),
        name="sum_and_spread",
    )(parts, note)


def exact_dot(left, one_hot, contract):
    total = None
    for _ in range(3):
        part = left.astype(BF16)
        left = left - part.astype(F32)
        term = lax.dot_general(part, one_hot, contract, preferred_element_type=F32)
        total = term if total is None else total + term
    return total


def finish_kernel(
    factor, grad_ref, act_ref, parity_ref, own_tag_ref, near_tag_ref, far_tag_ref, out_ref, tag_ref
):
    product = grad_ref[...] * act_ref[...].astype(F32)
    lane = lax.broadcasted_iota(jnp.int32, (CAP, TAG), 1) // 32
    odd = (parity_ref[0] == 1).astype(F32)
    own, near, far = (ref[...].astype(F32) for ref in (own_tag_ref, near_tag_ref, far_tag_ref))
    last = odd * far + (1.0 - odd) * own
    left = odd * own + (1.0 - odd) * far
    tag_ref[...] = jnp.zeros_like(tag_ref)
    tag_ref[:CAP] = jnp.where(lane == 1, near, 0.0).astype(BF16)
    tag_ref[CAP : 2 * CAP] = jnp.where(lane == 2, last, 0.0).astype(BF16)
    tag_ref[OWN : OWN + CAP] = jnp.where(lane == 3, own, 0.0).astype(BF16)
    by_column = exact_dot(product, tag_ref[...], (((1,), (0,)), ((), ())))[:CAP]
    by_row = (((0,), (0,)), ((), ()))
    pairs = exact_dot(by_column, left.astype(BF16), by_row)
    selves = exact_dot(by_column, own.astype(BF16), by_row)
    shape = (32, TAG)
    column = lax.broadcasted_iota(jnp.int32, shape, 0) // 4
    place = lax.broadcasted_iota(jnp.int32, shape, 1)
    out_ref[...] = factor * (
        jnp.where((place < 8) & (place != column), selves[96:128], 0.0)
        + jnp.where((place >= 8) & (place < 16), pairs[32:64], 0.0)
        + jnp.where((place >= 16) & (place < 24), pairs[64:96], 0.0)
    )


def finish(factor, grad_gram, act_gram, parity, tags):
    tag_at = tags[0].shape[1] // TAG - 1
    whole = pl.BlockSpec((TALL, WIDE), lambda step: (0, 0))
    tag = pl.BlockSpec((CAP, TAG), lambda step: (0, tag_at))
    return pl.pallas_call(
        functools.partial(finish_kernel, factor),
        grid=(1,),
        in_specs=[whole, whole, pl.BlockSpec(memory_space=pltpu.SMEM), tag, tag, tag],
        out_specs=pl.BlockSpec((32, TAG), lambda step: (0, 0)),
        out_shape=jax.ShapeDtypeStruct((32, TAG), F32),
        scratch_shapes=[pltpu.VMEM((WIDE, TAG), BF16)],
        compiler_params=pltpu.CompilerParams(vmem_limit_bytes=VMEM_LIMIT),
        name="finish",
    )(grad_gram, act_gram, parity, *tags)


def far_swap(value):
    count = lax.axis_size("ex")
    pairs = [(e, (e + (2 if e % 2 else -2)) % count) for e in range(count)]
    return lax.ppermute(value, "ex", pairs)


def near_swap(value):
    count = lax.axis_size("ex")
    return lax.ppermute(value, "ex", [(e, e ^ 1) for e in range(count)])


def sum_over_width(value, note):
    parts = lax.axis_size("width")
    split = value.reshape(parts, TALL // parts, WIDE)
    spread, most = sum_and_spread(lax.all_to_all(split, "width", 0, 0), note)
    return lax.all_to_all(spread, "width", 0, 0).reshape(TALL, WIDE), most


def local(activations, gradients, act_scale, grad_scale, counts, loss_mask):
    ex_local, tok_slots = loss_mask.shape
    row_count = ex_local * tok_slots
    own_acts = activations[0].reshape(row_count, -1)
    own_grads = gradients[0].reshape(row_count, -1)
    positions = lax.broadcasted_iota(jnp.int32, (ex_local, tok_slots), 1)
    token_weight = (positions < counts[:, None]).astype(jnp.int32) * loss_mask
    weight_rows = token_weight.astype(F32).reshape(row_count)
    parity = (lax.axis_index("ex") % 2).astype(jnp.int32).reshape(1)
    factor = 1.0 / (math.sqrt(D * FF) * tok_slots)

    acts, pick, over = pack_acts(counts, loss_mask, own_acts)
    far_acts, near_acts = far_swap(acts), near_swap(acts)
    grads = pack_grads(pick, own_grads, near_acts)
    far_grads, near_grads = far_swap(grads), near_swap(grads)
    over_all = lax.all_to_all(over, "ex", 0, 0, tiled=True)

    act_gram = gram(acts, near_acts, far_acts, act_scale, parity, 300)
    act_gram, most = sum_over_width(act_gram, over_all)
    crowded = most[0, 0] > 0.0
    grad_gram = gram(grads, near_grads, far_grads, grad_scale, parity, 1)
    scores = finish(factor, grad_gram, act_gram, parity, (acts, near_acts, far_acts))
    mine = lax.all_to_all(scores, ("layer", "width"), 0, 0, tiled=True).sum(axis=0)
    ahead = from_behind(mine, "ex", 2)
    place = lax.broadcasted_iota(jnp.int32, mine.shape, 0)
    kept = jnp.where((place < 8) | (parity[0] == 1), mine, ahead)
    quick = kept[: 8 * (HOPS + 1)].reshape(HOPS + 1, ex_local, 1)
    return lax.cond(
        crowded,
        lambda: plain(activations, gradients, act_scale, grad_scale, weight_rows, tok_slots),
        lambda: quick,
    )


def solution(mesh):
    in_specs = (
        P("layer", "ex", None, "width"),
        P("layer", "ex", None, "width"),
        P("layer", "width"),
        P("layer", "width"),
        P("ex"),
        P("ex", None),
    )
    out_specs = P(None, "ex", "layer")
    return jax.shard_map(local, mesh=mesh, in_specs=in_specs, out_specs=out_specs, check_vma=False)
```

```python
import functools
import math

import jax
import jax.numpy as jnp
from jax import lax
from jax.experimental import pallas as pl
from jax.experimental.pallas import tpu as pltpu
from jax.sharding import PartitionSpec as P

D = 8192
FF = 28672
HOPS = 2
CAP = 176
TALL = 192
OWN = 384
WIDE = 640
TAG = 128
PART = 1792
BF16 = jnp.bfloat16
F32 = jnp.float32
VMEM_LIMIT = 24 * 1024 * 1024


def from_behind(value, axis, steps):
    count = lax.axis_size(axis)
    pairs = [(source, (source + steps) % count) for source in range(count)]
    return lax.ppermute(value, axis, pairs)


def butterfly_sum(value, axis):
    count, step = lax.axis_size(axis), 1
    while step < count:
        value = value + lax.ppermute(value, axis, [(place, place ^ step) for place in range(count)])
        step *= 2
    return value


def plain(activations, gradients, act_scale, grad_scale, weight_rows, tok_slots):
    row_count = weight_rows.shape[0]
    ex_local = row_count // tok_slots
    own_acts = activations[0].reshape(row_count, -1)
    own_grads = gradients[0].reshape(row_count, -1)
    stat_acts = (own_acts.astype(F32) * act_scale[0]).astype(BF16)
    stat_grads = (own_grads.astype(F32) * grad_scale[0]).astype(BF16)
    factor = 1.0 / (math.sqrt(D * FF) * tok_slots)
    contract = (((1,), (1,)), ((), ()))

    def pair_scores(partner):
        move_acts, move_grads, move_weight = partner
        act_gram = lax.dot_general(stat_acts, move_acts, contract, preferred_element_type=F32)
        grad_gram = lax.dot_general(stat_grads, move_grads, contract, preferred_element_type=F32)
        act_gram, grad_gram = butterfly_sum(act_gram, "width"), butterfly_sum(grad_gram, "width")
        product = act_gram * grad_gram * weight_rows[:, None] * move_weight.astype(F32)[None, :]
        return product.reshape(ex_local, tok_slots, ex_local, tok_slots).sum(axis=(1, 3)) * factor

    partner = (own_acts, own_grads, weight_rows.astype(BF16))
    scores = [pair_scores(partner)]
    for distance in range(HOPS):
        partner = tuple(from_behind(value, "ex", 1) for value in partner)
        scores.append(pair_scores(partner))
    local_ex = lax.broadcasted_iota(jnp.int32, (ex_local, ex_local), 0)
    column_ex = lax.broadcasted_iota(jnp.int32, (ex_local, ex_local), 1)
    scores[0] = scores[0] * (local_ex != column_ex).astype(F32)
    summed = butterfly_sum(jnp.stack(scores), "layer")
    column = lax.axis_index("layer") * (ex_local // lax.axis_size("layer"))
    return lax.dynamic_slice_in_dim(summed, column, ex_local // lax.axis_size("layer"), axis=2)


def token_weights(counts_ref, mask_ref):
    ex_local, tok_slots = mask_ref.shape
    rows = ex_local * tok_slots
    position = lax.broadcasted_iota(jnp.int32, (ex_local, tok_slots), 1)
    example = lax.broadcasted_iota(jnp.int32, (ex_local, tok_slots), 0)
    filled = jnp.zeros((ex_local, tok_slots), jnp.int32)
    for place in range(ex_local):
        filled = jnp.where(example == place, counts_ref[place], filled)
    weight = jnp.where((position < filled) & (mask_ref[...] == 1), 1.0, 0.0)
    lane = lax.broadcasted_iota(jnp.int32, (tok_slots, rows), 1)
    slot = lax.broadcasted_iota(jnp.int32, (tok_slots, rows), 0)
    spread = jnp.where(lane % tok_slots == slot, 1.0, 0.0).astype(BF16)
    wide = jnp.dot(weight.astype(BF16), spread, preferred_element_type=F32)
    owner = lax.broadcasted_iota(jnp.int32, (ex_local, rows), 1) // tok_slots
    row = lax.broadcasted_iota(jnp.int32, (ex_local, rows), 0)
    return jnp.sum(jnp.where(owner == row, wide, 0.0), axis=0, keepdims=True)


def pack_acts_kernel(
    counts_at, mask_at, rows_at, packed_ref, pick_ref, over_ref, counts_ref, mask_ref, rows_ref, done
):
    copies = [
        pltpu.make_async_copy(source, target, done.at[place])
        for place, (source, target) in enumerate(
            ((counts_at, counts_ref), (mask_at, mask_ref), (rows_at, rows_ref))
        )
    ]
    for copy in copies:
        copy.start()
    copies[0].wait()
    copies[1].wait()
    features, rows = rows_ref.shape[1], rows_ref.shape[0]
    tok_slots = mask_ref.shape[1]
    weights = token_weights(counts_ref, mask_ref)
    before = lax.broadcasted_iota(jnp.int32, (rows, rows), 0)
    upto = lax.broadcasted_iota(jnp.int32, (rows, rows), 1)
    ramp = jnp.where(before <= upto, 1.0, 0.0).astype(BF16)
    lifted = jnp.broadcast_to(weights, (16, rows)).astype(BF16)
    rank = jnp.dot(lifted, ramp, preferred_element_type=F32)[0:1]
    slot = lax.broadcasted_iota(jnp.int32, (CAP, rows), 0).astype(F32) + 1.0
    pick = (jnp.where(slot == rank, 1.0, 0.0) * weights).astype(BF16)
    pick_ref[...] = pick
    total = jnp.broadcast_to(jnp.sum(weights, axis=1, keepdims=True), over_ref.shape)
    over_ref[...] = jnp.where(total > CAP, 1.0, 0.0)
    copies[2].wait()
    packed_ref[:, :features] = jnp.dot(pick, rows_ref[...], preferred_element_type=F32).astype(BF16)
    shape = (rows, TAG)
    example = lax.broadcasted_iota(jnp.int32, shape, 0) // tok_slots
    lane = lax.broadcasted_iota(jnp.int32, shape, 1)
    short = jnp.where(lane % 8 == example, 1.0, 0.0)
    long = jnp.where((lane % 32) // 4 == example, 1.0, 0.0)
    tags = jnp.where(lane < 32, short, long).astype(BF16)
    packed_ref[:, features:] = jnp.dot(pick, tags, preferred_element_type=F32).astype(BF16)


def pack_acts(counts, mask, rows):
    count, features = rows.shape
    vmem = pl.BlockSpec(memory_space=pltpu.VMEM)
    return pl.pallas_call(
        pack_acts_kernel,
        in_specs=[pl.BlockSpec(memory_space=pltpu.HBM)] * 3,
        out_specs=[vmem, vmem, vmem],
        scratch_shapes=[
            pltpu.SMEM(counts.shape, jnp.int32),
            pltpu.VMEM(mask.shape, jnp.int32),
            pltpu.VMEM(rows.shape, BF16),
            pltpu.SemaphoreType.DMA((3,)),
        ],
        out_shape=[
            jax.ShapeDtypeStruct((CAP, features + TAG), BF16),
            jax.ShapeDtypeStruct((CAP, count), BF16),
            jax.ShapeDtypeStruct((16, TAG), F32),
        ],
        compiler_params=pltpu.CompilerParams(vmem_limit_bytes=VMEM_LIMIT),
        cost_estimate=pl.CostEstimate(
            flops=2 * CAP * count * features, bytes_accessed=4 * count * features, transcendentals=0
        ),
        name="pack_acts",
    )(counts, mask, rows)


def pack_grads_kernel(
    pick_ref, rows_at, after_at, head_at, tail_at, rows_ref, packed_ref, came, left
):
    del after_at
    head = head_at.shape[1]
    firsts = range(0, rows_ref.shape[1], PART)
    parts = [pl.ds(first, PART) for first in firsts]
    loads = [
        pltpu.make_async_copy(rows_at.at[:, part], rows_ref.at[:, part], came.at[place])
        for place, part in enumerate(parts)
    ]
    targets = [
        head_at.at[:, pl.ds(first, PART)] if first < head else tail_at.at[:, pl.ds(first - head, PART)]
        for first in firsts
    ]
    stores = [
        pltpu.make_async_copy(packed_ref.at[:, part], target, left.at[place])
        for place, (part, target) in enumerate(zip(parts, targets))
    ]
    for load in loads:
        load.start()
    for part, load, store in zip(parts, loads, stores):
        load.wait()
        packed_ref[:, part] = jnp.dot(
            pick_ref[...], rows_ref[:, part], preferred_element_type=F32
        ).astype(BF16)
        store.start()
    for store in stores:
        store.wait()


def pack_grads(pick, rows, after):
    count, features = rows.shape
    anywhere = pl.BlockSpec(memory_space=pl.ANY)
    return pl.pallas_call(
        pack_grads_kernel,
        in_specs=[pl.BlockSpec(memory_space=pltpu.VMEM), anywhere, anywhere],
        out_specs=[anywhere, anywhere],
        out_shape=[
            jax.ShapeDtypeStruct((CAP, features - PART), BF16),
            jax.ShapeDtypeStruct((CAP, PART), BF16),
        ],
        scratch_shapes=[
            pltpu.VMEM((count, features), BF16),
            pltpu.VMEM((CAP, features), BF16),
            pltpu.SemaphoreType.DMA((features // PART,)),
            pltpu.SemaphoreType.DMA((features // PART,)),
        ],
        compiler_params=pltpu.CompilerParams(vmem_limit_bytes=VMEM_LIMIT),
        cost_estimate=pl.CostEstimate(
            flops=40 * CAP * count * features, bytes_accessed=4 * count * features, transcendentals=0
        ),
        name="pack_grads",
    )(pick, rows, after)


def gram_kernel(far_ref, near_ref, own_ref, scale_ref, parity_ref, gram_ref):
    contract = (((1,), (1,)), ((), ()))
    features = scale_ref.shape[1]
    gram_ref[...] = jnp.zeros_like(gram_ref)

    def read(ref):
        return ref[:, :features]

    def scaled(ref):
        return (read(ref).astype(F32) * scale_ref[...]).astype(BF16)

    def put(columns, left, right):
        gram_ref[:CAP, columns] = lax.dot_general(
            left, right, contract, preferred_element_type=F32
        ).astype(BF16)

    pair, alone = slice(0, 2 * CAP), slice(OWN, OWN + CAP)

    @pl.when(parity_ref[0] == 1)
    def _():
        left = scaled(own_ref)
        put(pair, left, jnp.concatenate([read(near_ref), read(far_ref)], axis=0))
        put(alone, left, read(own_ref))

    @pl.when(parity_ref[0] == 0)
    def _():
        put(pair, scaled(far_ref), jnp.concatenate([read(near_ref), read(own_ref)], axis=0))
        put(alone, scaled(own_ref), read(own_ref))


def gram(own, near, far, scale, parity):
    vmem = pl.BlockSpec(memory_space=pltpu.VMEM)
    return pl.pallas_call(
        gram_kernel,
        in_specs=[vmem, vmem, vmem, vmem, pl.BlockSpec(memory_space=pltpu.SMEM)],
        out_specs=vmem,
        out_shape=jax.ShapeDtypeStruct((TALL, WIDE), BF16),
        compiler_params=pltpu.CompilerParams(vmem_limit_bytes=VMEM_LIMIT),
        cost_estimate=pl.CostEstimate(
            flops=1800 * 256 * 256 * scale.shape[1], bytes_accessed=6 * CAP * scale.shape[1], transcendentals=0
        ),
        name="gram",
    )(far, near, own, scale, parity)


def add_grams(gram_ref, far_ref, near_ref, own_ref, scale_ref, parity_ref, part):
    contract = (((1,), (1,)), ((), ()))

    def scaled(ref):
        return (ref[:, part].astype(F32) * scale_ref[:, part]).astype(BF16)

    def add(columns, left, right):
        gram_ref[:CAP, columns] += lax.dot_general(left, right, contract, preferred_element_type=F32)

    pair, alone = slice(0, 2 * CAP), slice(OWN, OWN + CAP)

    @pl.when(parity_ref[0] == 1)
    def _():
        left = scaled(own_ref)
        add(pair, left, jnp.concatenate([near_ref[:, part], far_ref[:, part]], axis=0))
        add(alone, left, own_ref[:, part])

    @pl.when(parity_ref[0] == 0)
    def _():
        add(pair, scaled(far_ref), jnp.concatenate([near_ref[:, part], own_ref[:, part]], axis=0))
        add(alone, scaled(own_ref), own_ref[:, part])


def head_kernel(
    far_at, near_at, own_at, scale_ref, parity_ref, gram_ref, far_ref, near_ref, own_ref, came
):
    parts = [pl.ds(first, PART) for first in range(0, own_at.shape[1], PART)]
    blocks = ((far_at, far_ref), (near_at, near_ref), (own_at, own_ref))
    loads = [
        [
            pltpu.make_async_copy(source.at[:, part], target.at[:, part], came.at[place, which])
            for which, (source, target) in enumerate(blocks)
        ]
        for place, part in enumerate(parts)
    ]
    for row in loads:
        for load in row:
            load.start()
    gram_ref[...] = jnp.zeros_like(gram_ref)
    for part, row in zip(parts, loads):
        for load in row:
            load.wait()
        add_grams(gram_ref, far_ref, near_ref, own_ref, scale_ref, parity_ref, part)


def head_grams(own, near, far, scale, parity):
    features = own.shape[1]
    anywhere = pl.BlockSpec(memory_space=pl.ANY)
    vmem = pl.BlockSpec(memory_space=pltpu.VMEM)
    return pl.pallas_call(
        head_kernel,
        in_specs=[anywhere, anywhere, anywhere, vmem, pl.BlockSpec(memory_space=pltpu.SMEM)],
        out_specs=vmem,
        out_shape=jax.ShapeDtypeStruct((TALL, WIDE), F32),
        scratch_shapes=[pltpu.VMEM((CAP, features), BF16)] * 3
        + [pltpu.SemaphoreType.DMA((features // PART, 3))],
        compiler_params=pltpu.CompilerParams(vmem_limit_bytes=VMEM_LIMIT),
        cost_estimate=pl.CostEstimate(
            flops=6 * 256 * 256 * features, bytes_accessed=6 * CAP * features, transcendentals=0
        ),
        name="head_grams",
    )(far, near, own, scale, parity)


def spread_kernel(parts_ref, note_ref, out_ref, said_ref):
    total = parts_ref[0].astype(F32)
    for part in range(1, parts_ref.shape[0]):
        total = total + parts_ref[part].astype(F32)
    rounded = total.astype(BF16)
    for part in range(out_ref.shape[0]):
        out_ref[part] = rounded
    said_ref[...] = jnp.max(note_ref[...], axis=0, keepdims=True)


def sum_and_spread(parts, note):
    return pl.pallas_call(
        spread_kernel,
        out_shape=[
            jax.ShapeDtypeStruct(parts.shape, BF16),
            jax.ShapeDtypeStruct((1, note.shape[1]), F32),
        ],
        compiler_params=pltpu.CompilerParams(vmem_limit_bytes=VMEM_LIMIT),
        name="sum_and_spread",
    )(parts, note)


def exact_dot(left, one_hot, contract):
    total = None
    for _ in range(3):
        part = left.astype(BF16)
        left = left - part.astype(F32)
        term = lax.dot_general(part, one_hot, contract, preferred_element_type=F32)
        total = term if total is None else total + term
    return total


def finish_kernel(
    factor, far_ref, near_ref, own_ref, scale_ref, head_ref, act_ref, parity_ref,
    own_tag_ref, near_tag_ref, far_tag_ref, out_ref, gram_ref, tag_ref,
):
    gram_ref[...] = head_ref[...]
    add_grams(gram_ref, far_ref, near_ref, own_ref, scale_ref, parity_ref, slice(None))
    product = gram_ref[...] * act_ref[...].astype(F32)
    lane = lax.broadcasted_iota(jnp.int32, (CAP, TAG), 1) // 32
    odd = (parity_ref[0] == 1).astype(F32)
    own, near, far = (ref[...].astype(F32) for ref in (own_tag_ref, near_tag_ref, far_tag_ref))
    last = odd * far + (1.0 - odd) * own
    left = odd * own + (1.0 - odd) * far
    tag_ref[...] = jnp.zeros_like(tag_ref)
    tag_ref[:CAP] = jnp.where(lane == 1, near, 0.0).astype(BF16)
    tag_ref[CAP : 2 * CAP] = jnp.where(lane == 2, last, 0.0).astype(BF16)
    tag_ref[OWN : OWN + CAP] = jnp.where(lane == 3, own, 0.0).astype(BF16)
    by_column = exact_dot(product, tag_ref[...], (((1,), (0,)), ((), ())))[:CAP]
    by_row = (((0,), (0,)), ((), ()))
    pairs = exact_dot(by_column, left.astype(BF16), by_row)
    selves = exact_dot(by_column, own.astype(BF16), by_row)
    shape = (32, TAG)
    column = lax.broadcasted_iota(jnp.int32, shape, 0) // 4
    place = lax.broadcasted_iota(jnp.int32, shape, 1)
    out_ref[...] = factor * (
        jnp.where((place < 8) & (place != column), selves[96:128], 0.0)
        + jnp.where((place >= 8) & (place < 16), pairs[32:64], 0.0)
        + jnp.where((place >= 16) & (place < 24), pairs[64:96], 0.0)
    )


def finish(factor, own, near, far, scale, head_gram, act_gram, parity, tags):
    tag_at = tags[0].shape[1] // TAG - 1
    last = scale.shape[1] // PART - 1
    block = pl.BlockSpec((CAP, PART), lambda step: (0, 0))
    whole = pl.BlockSpec((TALL, WIDE), lambda step: (0, 0))
    tag = pl.BlockSpec((CAP, TAG), lambda step: (0, tag_at))
    return pl.pallas_call(
        functools.partial(finish_kernel, factor),
        grid=(1,),
        in_specs=[
            block,
            block,
            block,
            pl.BlockSpec((1, PART), lambda step: (0, last)),
            whole,
            whole,
            pl.BlockSpec(memory_space=pltpu.SMEM),
            tag,
            tag,
            tag,
        ],
        out_specs=pl.BlockSpec((32, TAG), lambda step: (0, 0)),
        out_shape=jax.ShapeDtypeStruct((32, TAG), F32),
        scratch_shapes=[pltpu.VMEM((TALL, WIDE), F32), pltpu.VMEM((WIDE, TAG), BF16)],
        compiler_params=pltpu.CompilerParams(vmem_limit_bytes=VMEM_LIMIT),
        name="finish",
    )(far, near, own, scale, head_gram, act_gram, parity, *tags)


def far_swap(value):
    count = lax.axis_size("ex")
    pairs = [(e, (e + (2 if e % 2 else -2)) % count) for e in range(count)]
    return lax.ppermute(value, "ex", pairs)


def near_swap(value):
    count = lax.axis_size("ex")
    return lax.ppermute(value, "ex", [(e, e ^ 1) for e in range(count)])


def sum_over_width(value, note):
    parts = lax.axis_size("width")
    split = value.reshape(parts, TALL // parts, WIDE)
    spread, most = sum_and_spread(lax.all_to_all(split, "width", 0, 0), note)
    return lax.all_to_all(spread, "width", 0, 0).reshape(TALL, WIDE), most


def local(activations, gradients, act_scale, grad_scale, counts, loss_mask):
    ex_local, tok_slots = loss_mask.shape
    row_count = ex_local * tok_slots
    own_acts = activations[0].reshape(row_count, -1)
    own_grads = gradients[0].reshape(row_count, -1)
    positions = lax.broadcasted_iota(jnp.int32, (ex_local, tok_slots), 1)
    token_weight = (positions < counts[:, None]).astype(jnp.int32) * loss_mask
    weight_rows = token_weight.astype(F32).reshape(row_count)
    parity = (lax.axis_index("ex") % 2).astype(jnp.int32).reshape(1)
    factor = 1.0 / (math.sqrt(D * FF) * tok_slots)

    acts, pick, over = pack_acts(counts, loss_mask, own_acts)
    far_acts, near_acts = far_swap(acts), near_swap(acts)
    head, tail = pack_grads(pick, own_grads, near_acts)
    far_head, far_tail = far_swap(head), far_swap(tail)
    near_head, near_tail = near_swap(head), near_swap(tail)

    over_all = lax.all_to_all(over, "ex", 0, 0, tiled=True)
    act_gram = gram(acts, near_acts, far_acts, act_scale, parity)
    act_gram, most = sum_over_width(act_gram, over_all)
    crowded = most[0, 0] > 0.0
    head_gram = head_grams(head, near_head, far_head, grad_scale, parity)
    scores = finish(
        factor, tail, near_tail, far_tail, grad_scale, head_gram, act_gram, parity,
        (acts, near_acts, far_acts),
    )
    mine = lax.all_to_all(scores, ("layer", "width"), 0, 0, tiled=True).sum(axis=0)
    ahead = from_behind(mine, "ex", 2)
    place = lax.broadcasted_iota(jnp.int32, mine.shape, 0)
    kept = jnp.where((place < 8) | (parity[0] == 1), mine, ahead)
    quick = kept[: 8 * (HOPS + 1)].reshape(HOPS + 1, ex_local, 1)
    return lax.cond(
        crowded,
        lambda: plain(activations, gradients, act_scale, grad_scale, weight_rows, tok_slots),
        lambda: quick,
    )


def solution(mesh):
    in_specs = (
        P("layer", "ex", None, "width"),
        P("layer", "ex", None, "width"),
        P("layer", "width"),
        P("layer", "width"),
        P("ex"),
        P("ex", None),
    )
    out_specs = P(None, "ex", "layer")
    return jax.shard_map(local, mesh=mesh, in_specs=in_specs, out_specs=out_specs, check_vma=False)
```

```python
import functools
import math

import jax
import jax.numpy as jnp
from jax import lax
from jax.experimental import pallas as pl
from jax.experimental.pallas import tpu as pltpu
from jax.sharding import PartitionSpec as P

D = 8192
FF = 28672
HOPS = 2
CAPS = (176, 192)
TALL = 192
OWN = 384
WIDE = 640
TAG = 128
PART = 1792
BF16 = jnp.bfloat16
F32 = jnp.float32
VMEM_LIMIT = 24 * 1024 * 1024


def from_behind(value, axis, steps):
    count = lax.axis_size(axis)
    pairs = [(source, (source + steps) % count) for source in range(count)]
    return lax.ppermute(value, axis, pairs)


def butterfly_sum(value, axis):
    count, step = lax.axis_size(axis), 1
    while step < count:
        value = value + lax.ppermute(value, axis, [(place, place ^ step) for place in range(count)])
        step *= 2
    return value


def plain(activations, gradients, act_scale, grad_scale, weight_rows, tok_slots):
    row_count = weight_rows.shape[0]
    ex_local = row_count // tok_slots
    own_acts = activations[0].reshape(row_count, -1)
    own_grads = gradients[0].reshape(row_count, -1)
    stat_acts = (own_acts.astype(F32) * act_scale[0]).astype(BF16)
    stat_grads = (own_grads.astype(F32) * grad_scale[0]).astype(BF16)
    factor = 1.0 / (math.sqrt(D * FF) * tok_slots)
    contract = (((1,), (1,)), ((), ()))

    partner = (own_acts, own_grads, weight_rows.astype(BF16))
    grams, move_weights = [], []
    for distance in range(HOPS + 1):
        if distance:
            partner = tuple(from_behind(value, "ex", 1) for value in partner)
        for stat, move in ((stat_acts, partner[0]), (stat_grads, partner[1])):
            grams.append(lax.dot_general(stat, move, contract, preferred_element_type=F32))
        move_weights.append(partner[2].astype(F32))
    grams = butterfly_sum(jnp.stack(grams), "width")
    scores = []
    for distance, move_weight in enumerate(move_weights):
        product = grams[2 * distance] * grams[2 * distance + 1]
        product = product * weight_rows[:, None] * move_weight[None, :]
        product = product.reshape(ex_local, tok_slots, ex_local, tok_slots)
        scores.append(product.sum(axis=(1, 3)) * factor)
    local_ex = lax.broadcasted_iota(jnp.int32, (ex_local, ex_local), 0)
    column_ex = lax.broadcasted_iota(jnp.int32, (ex_local, ex_local), 1)
    scores[0] = scores[0] * (local_ex != column_ex).astype(F32)
    summed = butterfly_sum(jnp.stack(scores), "layer")
    column = lax.axis_index("layer") * (ex_local // lax.axis_size("layer"))
    return lax.dynamic_slice_in_dim(summed, column, ex_local // lax.axis_size("layer"), axis=2)


def token_weights(counts_ref, mask_ref):
    ex_local, tok_slots = mask_ref.shape
    rows = ex_local * tok_slots
    position = lax.broadcasted_iota(jnp.int32, (ex_local, tok_slots), 1)
    example = lax.broadcasted_iota(jnp.int32, (ex_local, tok_slots), 0)
    filled = jnp.zeros((ex_local, tok_slots), jnp.int32)
    for place in range(ex_local):
        filled = jnp.where(example == place, counts_ref[place], filled)
    weight = jnp.where((position < filled) & (mask_ref[...] == 1), 1.0, 0.0)
    lane = lax.broadcasted_iota(jnp.int32, (tok_slots, rows), 1)
    slot = lax.broadcasted_iota(jnp.int32, (tok_slots, rows), 0)
    spread = jnp.where(lane % tok_slots == slot, 1.0, 0.0).astype(BF16)
    wide = jnp.dot(weight.astype(BF16), spread, preferred_element_type=F32)
    owner = lax.broadcasted_iota(jnp.int32, (ex_local, rows), 1) // tok_slots
    row = lax.broadcasted_iota(jnp.int32, (ex_local, rows), 0)
    return jnp.sum(jnp.where(owner == row, wide, 0.0), axis=0, keepdims=True)


def pack_acts_kernel(
    counts_at, mask_at, rows_at, packed_ref, pick_ref, many_ref, counts_ref, mask_ref, rows_ref, done
):
    copies = [
        pltpu.make_async_copy(source, target, done.at[place])
        for place, (source, target) in enumerate(
            ((counts_at, counts_ref), (mask_at, mask_ref), (rows_at, rows_ref))
        )
    ]
    for copy in copies:
        copy.start()
    copies[0].wait()
    copies[1].wait()
    features, rows = rows_ref.shape[1], rows_ref.shape[0]
    tok_slots = mask_ref.shape[1]
    weights = token_weights(counts_ref, mask_ref)
    before = lax.broadcasted_iota(jnp.int32, (rows, rows), 0)
    upto = lax.broadcasted_iota(jnp.int32, (rows, rows), 1)
    ramp = jnp.where(before <= upto, 1.0, 0.0).astype(BF16)
    lifted = jnp.broadcast_to(weights, (16, rows)).astype(BF16)
    rank = jnp.dot(lifted, ramp, preferred_element_type=F32)[0:1]
    slot = lax.broadcasted_iota(jnp.int32, (pick_ref.shape[0], rows), 0).astype(F32) + 1.0
    pick = (jnp.where(slot == rank, 1.0, 0.0) * weights).astype(BF16)
    pick_ref[...] = pick
    total = jnp.broadcast_to(jnp.sum(weights, axis=1, keepdims=True), many_ref.shape)
    many_ref[...] = total
    copies[2].wait()
    packed_ref[:, :features] = jnp.dot(pick, rows_ref[...], preferred_element_type=F32).astype(BF16)
    shape = (rows, TAG)
    example = lax.broadcasted_iota(jnp.int32, shape, 0) // tok_slots
    lane = lax.broadcasted_iota(jnp.int32, shape, 1)
    short = jnp.where(lane % 8 == example, 1.0, 0.0)
    long = jnp.where((lane % 32) // 4 == example, 1.0, 0.0)
    tags = jnp.where(lane < 32, short, long).astype(BF16)
    packed_ref[:, features:] = jnp.dot(pick, tags, preferred_element_type=F32).astype(BF16)


def pack_acts(counts, mask, rows, cap):
    count, features = rows.shape
    vmem = pl.BlockSpec(memory_space=pltpu.VMEM)
    return pl.pallas_call(
        pack_acts_kernel,
        in_specs=[pl.BlockSpec(memory_space=pltpu.HBM)] * 3,
        out_specs=[vmem, vmem, vmem],
        scratch_shapes=[
            pltpu.SMEM(counts.shape, jnp.int32),
            pltpu.VMEM(mask.shape, jnp.int32),
            pltpu.VMEM(rows.shape, BF16),
            pltpu.SemaphoreType.DMA((3,)),
        ],
        out_shape=[
            jax.ShapeDtypeStruct((cap, features + TAG), BF16),
            jax.ShapeDtypeStruct((cap, count), BF16),
            jax.ShapeDtypeStruct((16, TAG), F32),
        ],
        compiler_params=pltpu.CompilerParams(vmem_limit_bytes=VMEM_LIMIT),
        cost_estimate=pl.CostEstimate(
            flops=2 * cap * count * features, bytes_accessed=4 * count * features, transcendentals=0
        ),
        name="pack_acts",
    )(counts, mask, rows)


def pack_grads_kernel(
    pick_ref, rows_at, after_at, head_at, tail_at, rows_ref, packed_ref, came, left
):
    del after_at
    head = head_at.shape[1]
    firsts = range(0, rows_ref.shape[1], PART)
    parts = [pl.ds(first, PART) for first in firsts]
    loads = [
        pltpu.make_async_copy(rows_at.at[:, part], rows_ref.at[:, part], came.at[place])
        for place, part in enumerate(parts)
    ]
    targets = [
        head_at.at[:, pl.ds(first, PART)] if first < head else tail_at.at[:, pl.ds(first - head, PART)]
        for first in firsts
    ]
    stores = [
        pltpu.make_async_copy(packed_ref.at[:, part], target, left.at[place])
        for place, (part, target) in enumerate(zip(parts, targets))
    ]
    for load in loads:
        load.start()
    for part, load, store in zip(parts, loads, stores):
        load.wait()
        packed_ref[:, part] = jnp.dot(
            pick_ref[...], rows_ref[:, part], preferred_element_type=F32
        ).astype(BF16)
        store.start()
    for store in stores:
        store.wait()


def pack_grads(pick, rows, after):
    count, features = rows.shape
    cap = pick.shape[0]
    anywhere = pl.BlockSpec(memory_space=pl.ANY)
    return pl.pallas_call(
        pack_grads_kernel,
        in_specs=[pl.BlockSpec(memory_space=pltpu.VMEM), anywhere, anywhere],
        out_specs=[anywhere, anywhere],
        out_shape=[
            jax.ShapeDtypeStruct((cap, features - PART), BF16),
            jax.ShapeDtypeStruct((cap, PART), BF16),
        ],
        scratch_shapes=[
            pltpu.VMEM((count, features), BF16),
            pltpu.VMEM((cap, features), BF16),
            pltpu.SemaphoreType.DMA((features // PART,)),
            pltpu.SemaphoreType.DMA((features // PART,)),
        ],
        compiler_params=pltpu.CompilerParams(vmem_limit_bytes=VMEM_LIMIT),
        cost_estimate=pl.CostEstimate(
            flops=40 * cap * count * features, bytes_accessed=4 * count * features, transcendentals=0
        ),
        name="pack_grads",
    )(pick, rows, after)


def gram_kernel(far_ref, near_ref, own_ref, scale_ref, parity_ref, gram_ref):
    contract = (((1,), (1,)), ((), ()))
    features = scale_ref.shape[1]
    cap = own_ref.shape[0]
    gram_ref[...] = jnp.zeros_like(gram_ref)

    def read(ref):
        return ref[:, :features]

    def scaled(ref):
        return (read(ref).astype(F32) * scale_ref[...]).astype(BF16)

    def put(columns, left, right):
        gram_ref[:cap, columns] = lax.dot_general(
            left, right, contract, preferred_element_type=F32
        ).astype(BF16)

    pair, alone = slice(0, 2 * cap), slice(OWN, OWN + cap)

    @pl.when(parity_ref[0] == 1)
    def _():
        left = scaled(own_ref)
        put(pair, left, jnp.concatenate([read(near_ref), read(far_ref)], axis=0))
        put(alone, left, read(own_ref))

    @pl.when(parity_ref[0] == 0)
    def _():
        put(pair, scaled(far_ref), jnp.concatenate([read(near_ref), read(own_ref)], axis=0))
        put(alone, scaled(own_ref), read(own_ref))


def gram(own, near, far, scale, parity):
    vmem = pl.BlockSpec(memory_space=pltpu.VMEM)
    return pl.pallas_call(
        gram_kernel,
        in_specs=[vmem, vmem, vmem, vmem, pl.BlockSpec(memory_space=pltpu.SMEM)],
        out_specs=vmem,
        out_shape=jax.ShapeDtypeStruct((TALL, WIDE), BF16),
        compiler_params=pltpu.CompilerParams(vmem_limit_bytes=VMEM_LIMIT),
        cost_estimate=pl.CostEstimate(
            flops=1800 * 256 * 256 * scale.shape[1], bytes_accessed=6 * own.shape[0] * scale.shape[1], transcendentals=0
        ),
        name="gram",
    )(far, near, own, scale, parity)


def add_grams(gram_ref, far_ref, near_ref, own_ref, scale_ref, parity_ref, part):
    contract = (((1,), (1,)), ((), ()))
    cap = own_ref.shape[0]

    def scaled(ref):
        return (ref[:, part].astype(F32) * scale_ref[:, part]).astype(BF16)

    def add(columns, left, right):
        gram_ref[:cap, columns] += lax.dot_general(left, right, contract, preferred_element_type=F32)

    pair, alone = slice(0, 2 * cap), slice(OWN, OWN + cap)

    @pl.when(parity_ref[0] == 1)
    def _():
        left = scaled(own_ref)
        add(pair, left, jnp.concatenate([near_ref[:, part], far_ref[:, part]], axis=0))
        add(alone, left, own_ref[:, part])

    @pl.when(parity_ref[0] == 0)
    def _():
        add(pair, scaled(far_ref), jnp.concatenate([near_ref[:, part], own_ref[:, part]], axis=0))
        add(alone, scaled(own_ref), own_ref[:, part])


def head_kernel(
    far_at, near_at, own_at, scale_ref, parity_ref, gram_ref, far_ref, near_ref, own_ref, came
):
    parts = [pl.ds(first, PART) for first in range(0, own_at.shape[1], PART)]
    blocks = ((far_at, far_ref), (near_at, near_ref), (own_at, own_ref))
    loads = [
        [
            pltpu.make_async_copy(source.at[:, part], target.at[:, part], came.at[place, which])
            for which, (source, target) in enumerate(blocks)
        ]
        for place, part in enumerate(parts)
    ]
    for row in loads:
        for load in row:
            load.start()
    gram_ref[...] = jnp.zeros_like(gram_ref)
    for part, row in zip(parts, loads):
        for load in row:
            load.wait()
        add_grams(gram_ref, far_ref, near_ref, own_ref, scale_ref, parity_ref, part)


def head_grams(own, near, far, scale, parity):
    cap, features = own.shape
    anywhere = pl.BlockSpec(memory_space=pl.ANY)
    vmem = pl.BlockSpec(memory_space=pltpu.VMEM)
    return pl.pallas_call(
        head_kernel,
        in_specs=[anywhere, anywhere, anywhere, vmem, pl.BlockSpec(memory_space=pltpu.SMEM)],
        out_specs=vmem,
        out_shape=jax.ShapeDtypeStruct((TALL, WIDE), F32),
        scratch_shapes=[pltpu.VMEM((cap, features), BF16)] * 3
        + [pltpu.SemaphoreType.DMA((features // PART, 3))],
        compiler_params=pltpu.CompilerParams(vmem_limit_bytes=VMEM_LIMIT),
        cost_estimate=pl.CostEstimate(
            flops=6 * 256 * 256 * features, bytes_accessed=6 * cap * features, transcendentals=0
        ),
        name="head_grams",
    )(far, near, own, scale, parity)


def spread_kernel(parts_ref, note_ref, out_ref, said_ref):
    total = parts_ref[0].astype(F32)
    for part in range(1, parts_ref.shape[0]):
        total = total + parts_ref[part].astype(F32)
    rounded = total.astype(BF16)
    for part in range(out_ref.shape[0]):
        out_ref[part] = rounded
    said_ref[...] = jnp.max(note_ref[...], axis=0, keepdims=True)


def sum_and_spread(parts, note):
    return pl.pallas_call(
        spread_kernel,
        out_shape=[
            jax.ShapeDtypeStruct(parts.shape, BF16),
            jax.ShapeDtypeStruct((1, note.shape[1]), F32),
        ],
        compiler_params=pltpu.CompilerParams(vmem_limit_bytes=VMEM_LIMIT),
        name="sum_and_spread",
    )(parts, note)


def exact_dot(left, one_hot, contract):
    total = None
    for _ in range(3):
        part = left.astype(BF16)
        left = left - part.astype(F32)
        term = lax.dot_general(part, one_hot, contract, preferred_element_type=F32)
        total = term if total is None else total + term
    return total


def finish_kernel(
    factor, far_ref, near_ref, own_ref, scale_ref, head_ref, act_ref, parity_ref,
    own_tag_ref, near_tag_ref, far_tag_ref, out_ref, gram_ref, tag_ref,
):
    cap = own_ref.shape[0]
    gram_ref[...] = head_ref[...]
    add_grams(gram_ref, far_ref, near_ref, own_ref, scale_ref, parity_ref, slice(None))
    product = gram_ref[...] * act_ref[...].astype(F32)
    lane = lax.broadcasted_iota(jnp.int32, (cap, TAG), 1) // 32
    odd = (parity_ref[0] == 1).astype(F32)
    own, near, far = (ref[...].astype(F32) for ref in (own_tag_ref, near_tag_ref, far_tag_ref))
    last = odd * far + (1.0 - odd) * own
    left = odd * own + (1.0 - odd) * far
    tag_ref[...] = jnp.zeros_like(tag_ref)
    tag_ref[:cap] = jnp.where(lane == 1, near, 0.0).astype(BF16)
    tag_ref[cap : 2 * cap] = jnp.where(lane == 2, last, 0.0).astype(BF16)
    tag_ref[OWN : OWN + cap] = jnp.where(lane == 3, own, 0.0).astype(BF16)
    by_column = exact_dot(product, tag_ref[...], (((1,), (0,)), ((), ())))[:cap]
    by_row = (((0,), (0,)), ((), ()))
    pairs = exact_dot(by_column, left.astype(BF16), by_row)
    selves = exact_dot(by_column, own.astype(BF16), by_row)
    shape = (32, TAG)
    column = lax.broadcasted_iota(jnp.int32, shape, 0) // 4
    place = lax.broadcasted_iota(jnp.int32, shape, 1)
    out_ref[...] = factor * (
        jnp.where((place < 8) & (place != column), selves[96:128], 0.0)
        + jnp.where((place >= 8) & (place < 16), pairs[32:64], 0.0)
        + jnp.where((place >= 16) & (place < 24), pairs[64:96], 0.0)
    )


def finish(factor, own, near, far, scale, head_gram, act_gram, parity, tags):
    tag_at = tags[0].shape[1] // TAG - 1
    last = scale.shape[1] // PART - 1
    cap = own.shape[0]
    block = pl.BlockSpec((cap, PART), lambda step: (0, 0))
    whole = pl.BlockSpec((TALL, WIDE), lambda step: (0, 0))
    tag = pl.BlockSpec((cap, TAG), lambda step: (0, tag_at))
    return pl.pallas_call(
        functools.partial(finish_kernel, factor),
        grid=(1,),
        in_specs=[
            block,
            block,
            block,
            pl.BlockSpec((1, PART), lambda step: (0, last)),
            whole,
            whole,
            pl.BlockSpec(memory_space=pltpu.SMEM),
            tag,
            tag,
            tag,
        ],
        out_specs=pl.BlockSpec((32, TAG), lambda step: (0, 0)),
        out_shape=jax.ShapeDtypeStruct((32, TAG), F32),
        scratch_shapes=[pltpu.VMEM((TALL, WIDE), F32), pltpu.VMEM((WIDE, TAG), BF16)],
        compiler_params=pltpu.CompilerParams(vmem_limit_bytes=VMEM_LIMIT),
        name="finish",
    )(far, near, own, scale, head_gram, act_gram, parity, *tags)


def far_swap(value):
    count = lax.axis_size("ex")
    pairs = [(e, (e + (2 if e % 2 else -2)) % count) for e in range(count)]
    return lax.ppermute(value, "ex", pairs)


def near_swap(value):
    count = lax.axis_size("ex")
    return lax.ppermute(value, "ex", [(e, e ^ 1) for e in range(count)])


def sum_over_width(value, note):
    parts = lax.axis_size("width")
    split = value.reshape(parts, TALL // parts, WIDE)
    spread, most = sum_and_spread(lax.all_to_all(split, "width", 0, 0), note)
    return lax.all_to_all(spread, "width", 0, 0).reshape(TALL, WIDE), most


def packed(cap, activations, gradients, act_scale, grad_scale, counts, loss_mask):
    ex_local, tok_slots = loss_mask.shape
    row_count = ex_local * tok_slots
    own_acts = activations[0].reshape(row_count, -1)
    own_grads = gradients[0].reshape(row_count, -1)
    parity = (lax.axis_index("ex") % 2).astype(jnp.int32).reshape(1)
    factor = 1.0 / (math.sqrt(D * FF) * tok_slots)

    acts, pick, many = pack_acts(counts, loss_mask, own_acts, cap)
    near_acts, far_acts = near_swap(acts), far_swap(acts)
    head, tail = pack_grads(pick, own_grads, near_acts)
    far_head, far_tail = far_swap(head), far_swap(tail)
    near_head, near_tail = near_swap(head), near_swap(tail)

    many = lax.all_to_all(many, "ex", 0, 0, tiled=True)
    act_gram = gram(acts, near_acts, far_acts, act_scale, parity)
    act_gram, most = sum_over_width(act_gram, many)
    head_gram = head_grams(head, near_head, far_head, grad_scale, parity)
    scores = finish(
        factor, tail, near_tail, far_tail, grad_scale, head_gram, act_gram, parity,
        (acts, near_acts, far_acts),
    )
    mine = lax.all_to_all(scores, ("layer", "width"), 0, 0, tiled=True).sum(axis=0)
    ahead = from_behind(mine, "ex", 2)
    place = lax.broadcasted_iota(jnp.int32, mine.shape, 0)
    kept = jnp.where((place < 8) | (parity[0] == 1), mine, ahead)
    return kept[: 8 * (HOPS + 1)].reshape(HOPS + 1, ex_local, 1), most[0, 0]


def local(activations, gradients, act_scale, grad_scale, counts, loss_mask):
    args = (activations, gradients, act_scale, grad_scale, counts, loss_mask)
    quick, most = packed(CAPS[0], *args)

    def whole():
        ex_local, tok_slots = loss_mask.shape
        positions = lax.broadcasted_iota(jnp.int32, (ex_local, tok_slots), 1)
        token_weight = (positions < counts[:, None]).astype(jnp.int32) * loss_mask
        weight_rows = token_weight.astype(F32).reshape(ex_local * tok_slots)
        return plain(activations, gradients, act_scale, grad_scale, weight_rows, tok_slots)

    def larger():
        return lax.cond(most > CAPS[1], whole, lambda: packed(CAPS[1], *args)[0])

    return lax.cond(most > CAPS[0], larger, lambda: quick)


def solution(mesh):
    in_specs = (
        P("layer", "ex", None, "width"),
        P("layer", "ex", None, "width"),
        P("layer", "width"),
        P("layer", "width"),
        P("ex"),
        P("ex", None),
    )
    out_specs = P(None, "ex", "layer")
    return jax.shard_map(local, mesh=mesh, in_specs=in_specs, out_specs=out_specs, check_vma=False)
```

```python
import functools
import math

import jax
import jax.numpy as jnp
from jax import lax
from jax.experimental import pallas as pl
from jax.experimental.pallas import tpu as pltpu
from jax.sharding import PartitionSpec as P

D = 8192
FF = 28672
HOPS = 2
CAPS = (176, 192)
TALL = 192
OWN = 384
WIDE = 640
TAG = 128
PART = 1792
BF16 = jnp.bfloat16
F32 = jnp.float32
VMEM_LIMIT = 24 * 1024 * 1024


def from_behind(value, axis, steps):
    count = lax.axis_size(axis)
    pairs = [(source, (source + steps) % count) for source in range(count)]
    return lax.ppermute(value, axis, pairs)


def butterfly_sum(value, axis):
    count, step = lax.axis_size(axis), 1
    while step < count:
        value = value + lax.ppermute(value, axis, [(place, place ^ step) for place in range(count)])
        step *= 2
    return value


def plain(activations, gradients, act_scale, grad_scale, weight_rows, tok_slots):
    row_count = weight_rows.shape[0]
    ex_local = row_count // tok_slots
    own_acts = activations[0].reshape(row_count, -1)
    own_grads = gradients[0].reshape(row_count, -1)
    stat_acts = (own_acts.astype(F32) * act_scale[0]).astype(BF16)
    stat_grads = (own_grads.astype(F32) * grad_scale[0]).astype(BF16)
    factor = 1.0 / (math.sqrt(D * FF) * tok_slots)
    contract = (((1,), (1,)), ((), ()))

    partner = (own_acts, own_grads, weight_rows.astype(BF16))
    grams, move_weights = [], []
    for distance in range(HOPS + 1):
        if distance:
            partner = tuple(from_behind(value, "ex", 1) for value in partner)
        for stat, move in ((stat_acts, partner[0]), (stat_grads, partner[1])):
            grams.append(lax.dot_general(stat, move, contract, preferred_element_type=F32))
        move_weights.append(partner[2].astype(F32))
    grams = butterfly_sum(jnp.stack(grams), "width")
    scores = []
    for distance, move_weight in enumerate(move_weights):
        product = grams[2 * distance] * grams[2 * distance + 1]
        product = product * weight_rows[:, None] * move_weight[None, :]
        product = product.reshape(ex_local, tok_slots, ex_local, tok_slots)
        scores.append(product.sum(axis=(1, 3)) * factor)
    local_ex = lax.broadcasted_iota(jnp.int32, (ex_local, ex_local), 0)
    column_ex = lax.broadcasted_iota(jnp.int32, (ex_local, ex_local), 1)
    scores[0] = scores[0] * (local_ex != column_ex).astype(F32)
    summed = butterfly_sum(jnp.stack(scores), "layer")
    column = lax.axis_index("layer") * (ex_local // lax.axis_size("layer"))
    return lax.dynamic_slice_in_dim(summed, column, ex_local // lax.axis_size("layer"), axis=2)


def token_weights(counts_ref, mask_ref):
    ex_local, tok_slots = mask_ref.shape
    rows = ex_local * tok_slots
    position = lax.broadcasted_iota(jnp.int32, (ex_local, tok_slots), 1)
    example = lax.broadcasted_iota(jnp.int32, (ex_local, tok_slots), 0)
    filled = jnp.zeros((ex_local, tok_slots), jnp.int32)
    for place in range(ex_local):
        filled = jnp.where(example == place, counts_ref[place], filled)
    weight = jnp.where((position < filled) & (mask_ref[...] == 1), 1.0, 0.0)
    lane = lax.broadcasted_iota(jnp.int32, (tok_slots, rows), 1)
    slot = lax.broadcasted_iota(jnp.int32, (tok_slots, rows), 0)
    spread = jnp.where(lane % tok_slots == slot, 1.0, 0.0).astype(BF16)
    wide = jnp.dot(weight.astype(BF16), spread, preferred_element_type=F32)
    owner = lax.broadcasted_iota(jnp.int32, (ex_local, rows), 1) // tok_slots
    row = lax.broadcasted_iota(jnp.int32, (ex_local, rows), 0)
    return jnp.sum(jnp.where(owner == row, wide, 0.0), axis=0, keepdims=True)


def pack_acts_kernel(
    counts_at, mask_at, rows_at, packed_ref, pick_ref, many_ref, counts_ref, mask_ref, rows_ref, done
):
    copies = [
        pltpu.make_async_copy(source, target, done.at[place])
        for place, (source, target) in enumerate(
            ((counts_at, counts_ref), (mask_at, mask_ref), (rows_at, rows_ref))
        )
    ]
    for copy in copies:
        copy.start()
    copies[0].wait()
    copies[1].wait()
    features, rows = rows_ref.shape[1], rows_ref.shape[0]
    tok_slots = mask_ref.shape[1]
    weights = token_weights(counts_ref, mask_ref)
    before = lax.broadcasted_iota(jnp.int32, (rows, rows), 0)
    upto = lax.broadcasted_iota(jnp.int32, (rows, rows), 1)
    ramp = jnp.where(before <= upto, 1.0, 0.0).astype(BF16)
    lifted = jnp.broadcast_to(weights, (16, rows)).astype(BF16)
    rank = jnp.dot(lifted, ramp, preferred_element_type=F32)[0:1]
    slot = lax.broadcasted_iota(jnp.int32, (pick_ref.shape[0], rows), 0).astype(F32) + 1.0
    pick = (jnp.where(slot == rank, 1.0, 0.0) * weights).astype(BF16)
    pick_ref[...] = pick
    total = jnp.broadcast_to(jnp.sum(weights, axis=1, keepdims=True), many_ref.shape)
    many_ref[...] = total
    copies[2].wait()
    packed_ref[:, :features] = jnp.dot(pick, rows_ref[...], preferred_element_type=F32).astype(BF16)
    shape = (rows, TAG)
    example = lax.broadcasted_iota(jnp.int32, shape, 0) // tok_slots
    lane = lax.broadcasted_iota(jnp.int32, shape, 1)
    short = jnp.where(lane % 8 == example, 1.0, 0.0)
    long = jnp.where((lane % 32) // 4 == example, 1.0, 0.0)
    tags = jnp.where(lane < 32, short, long).astype(BF16)
    packed_ref[:, features:] = jnp.dot(pick, tags, preferred_element_type=F32).astype(BF16)


def pack_acts(counts, mask, rows, cap):
    count, features = rows.shape
    vmem = pl.BlockSpec(memory_space=pltpu.VMEM)
    return pl.pallas_call(
        pack_acts_kernel,
        in_specs=[pl.BlockSpec(memory_space=pltpu.HBM)] * 3,
        out_specs=[vmem, vmem, vmem],
        scratch_shapes=[
            pltpu.SMEM(counts.shape, jnp.int32),
            pltpu.VMEM(mask.shape, jnp.int32),
            pltpu.VMEM(rows.shape, BF16),
            pltpu.SemaphoreType.DMA((3,)),
        ],
        out_shape=[
            jax.ShapeDtypeStruct((cap, features + TAG), BF16),
            jax.ShapeDtypeStruct((cap, count), BF16),
            jax.ShapeDtypeStruct((16, TAG), F32),
        ],
        compiler_params=pltpu.CompilerParams(vmem_limit_bytes=VMEM_LIMIT),
        cost_estimate=pl.CostEstimate(
            flops=2 * cap * count * features, bytes_accessed=4 * count * features, transcendentals=0
        ),
        name="pack_acts",
    )(counts, mask, rows)


def pack_grads_kernel(
    pick_ref, rows_at, after_at, head_at, tail_at, rows_ref, packed_ref, came, left
):
    del after_at
    head = head_at.shape[1]
    firsts = range(0, rows_ref.shape[1], PART)
    parts = [pl.ds(first, PART) for first in firsts]
    loads = [
        pltpu.make_async_copy(rows_at.at[:, part], rows_ref.at[:, part], came.at[place])
        for place, part in enumerate(parts)
    ]
    targets = [
        head_at.at[:, pl.ds(first, PART)] if first < head else tail_at.at[:, pl.ds(first - head, PART)]
        for first in firsts
    ]
    stores = [
        pltpu.make_async_copy(packed_ref.at[:, part], target, left.at[place])
        for place, (part, target) in enumerate(zip(parts, targets))
    ]
    for load in loads:
        load.start()
    for part, load, store in zip(parts, loads, stores):
        load.wait()
        packed_ref[:, part] = jnp.dot(
            pick_ref[...], rows_ref[:, part], preferred_element_type=F32
        ).astype(BF16)
        store.start()
    for store in stores:
        store.wait()


def pack_grads(pick, rows, after):
    count, features = rows.shape
    cap = pick.shape[0]
    anywhere = pl.BlockSpec(memory_space=pl.ANY)
    return pl.pallas_call(
        pack_grads_kernel,
        in_specs=[pl.BlockSpec(memory_space=pltpu.VMEM), anywhere, anywhere],
        out_specs=[anywhere, anywhere],
        out_shape=[
            jax.ShapeDtypeStruct((cap, features - PART), BF16),
            jax.ShapeDtypeStruct((cap, PART), BF16),
        ],
        scratch_shapes=[
            pltpu.VMEM((count, features), BF16),
            pltpu.VMEM((cap, features), BF16),
            pltpu.SemaphoreType.DMA((features // PART,)),
            pltpu.SemaphoreType.DMA((features // PART,)),
        ],
        compiler_params=pltpu.CompilerParams(vmem_limit_bytes=VMEM_LIMIT),
        cost_estimate=pl.CostEstimate(
            flops=40 * cap * count * features, bytes_accessed=4 * count * features, transcendentals=0
        ),
        name="pack_grads",
    )(pick, rows, after)


def gram_kernel(far_ref, near_ref, own_ref, scale_ref, parity_ref, gram_ref):
    contract = (((1,), (1,)), ((), ()))
    features = scale_ref.shape[1]
    cap = own_ref.shape[0]
    gram_ref[...] = jnp.zeros_like(gram_ref)

    def read(ref):
        return ref[:, :features]

    def scaled(ref):
        return (read(ref).astype(F32) * scale_ref[...]).astype(BF16)

    def put(columns, left, right):
        gram_ref[:cap, columns] = lax.dot_general(
            left, right, contract, preferred_element_type=F32
        ).astype(BF16)

    pair, alone = slice(0, 2 * cap), slice(OWN, OWN + cap)

    @pl.when(parity_ref[0] == 1)
    def _():
        left = scaled(own_ref)
        put(pair, left, jnp.concatenate([read(near_ref), read(far_ref)], axis=0))
        put(alone, left, read(own_ref))

    @pl.when(parity_ref[0] == 0)
    def _():
        put(pair, scaled(far_ref), jnp.concatenate([read(near_ref), read(own_ref)], axis=0))
        put(alone, scaled(own_ref), read(own_ref))


def gram(own, near, far, scale, parity):
    vmem = pl.BlockSpec(memory_space=pltpu.VMEM)
    return pl.pallas_call(
        gram_kernel,
        in_specs=[vmem, vmem, vmem, vmem, pl.BlockSpec(memory_space=pltpu.SMEM)],
        out_specs=vmem,
        out_shape=jax.ShapeDtypeStruct((TALL, WIDE), BF16),
        compiler_params=pltpu.CompilerParams(vmem_limit_bytes=VMEM_LIMIT),
        cost_estimate=pl.CostEstimate(
            flops=1800 * 256 * 256 * scale.shape[1], bytes_accessed=6 * own.shape[0] * scale.shape[1], transcendentals=0
        ),
        name="gram",
    )(far, near, own, scale, parity)


def add_grams(gram_ref, far_ref, near_ref, own_ref, scale_ref, parity_ref, part):
    contract = (((1,), (1,)), ((), ()))
    cap = own_ref.shape[0]

    def scaled(ref):
        return (ref[:, part].astype(F32) * scale_ref[:, part]).astype(BF16)

    def add(columns, left, right):
        gram_ref[:cap, columns] += lax.dot_general(left, right, contract, preferred_element_type=F32)

    pair, alone = slice(0, 2 * cap), slice(OWN, OWN + cap)

    @pl.when(parity_ref[0] == 1)
    def _():
        left = scaled(own_ref)
        add(pair, left, jnp.concatenate([near_ref[:, part], far_ref[:, part]], axis=0))
        add(alone, left, own_ref[:, part])

    @pl.when(parity_ref[0] == 0)
    def _():
        add(pair, scaled(far_ref), jnp.concatenate([near_ref[:, part], own_ref[:, part]], axis=0))
        add(alone, scaled(own_ref), own_ref[:, part])


def head_kernel(
    far_at, near_at, own_at, scale_ref, parity_ref, gram_ref, far_ref, near_ref, own_ref, came
):
    parts = [pl.ds(first, PART) for first in range(0, own_at.shape[1], PART)]
    blocks = ((far_at, far_ref), (near_at, near_ref), (own_at, own_ref))
    loads = [
        [
            pltpu.make_async_copy(source.at[:, part], target.at[:, part], came.at[place, which])
            for which, (source, target) in enumerate(blocks)
        ]
        for place, part in enumerate(parts)
    ]
    for row in loads:
        for load in row:
            load.start()
    gram_ref[...] = jnp.zeros_like(gram_ref)
    for part, row in zip(parts, loads):
        for load in row:
            load.wait()
        add_grams(gram_ref, far_ref, near_ref, own_ref, scale_ref, parity_ref, part)


def head_grams(own, near, far, scale, parity):
    cap, features = own.shape
    anywhere = pl.BlockSpec(memory_space=pl.ANY)
    vmem = pl.BlockSpec(memory_space=pltpu.VMEM)
    return pl.pallas_call(
        head_kernel,
        in_specs=[anywhere, anywhere, anywhere, vmem, pl.BlockSpec(memory_space=pltpu.SMEM)],
        out_specs=vmem,
        out_shape=jax.ShapeDtypeStruct((TALL, WIDE), F32),
        scratch_shapes=[pltpu.VMEM((cap, features), BF16)] * 3
        + [pltpu.SemaphoreType.DMA((features // PART, 3))],
        compiler_params=pltpu.CompilerParams(vmem_limit_bytes=VMEM_LIMIT),
        cost_estimate=pl.CostEstimate(
            flops=6 * 256 * 256 * features, bytes_accessed=6 * cap * features, transcendentals=0
        ),
        name="head_grams",
    )(far, near, own, scale, parity)


def spread_kernel(parts_ref, note_ref, out_ref, said_ref):
    total = parts_ref[0].astype(F32)
    for part in range(1, parts_ref.shape[0]):
        total = total + parts_ref[part].astype(F32)
    rounded = total.astype(BF16)
    for part in range(out_ref.shape[0]):
        out_ref[part] = rounded
    said_ref[...] = jnp.max(note_ref[...], axis=0, keepdims=True)


def sum_and_spread(parts, note):
    return pl.pallas_call(
        spread_kernel,
        out_shape=[
            jax.ShapeDtypeStruct(parts.shape, BF16),
            jax.ShapeDtypeStruct((1, note.shape[1]), F32),
        ],
        compiler_params=pltpu.CompilerParams(vmem_limit_bytes=VMEM_LIMIT),
        name="sum_and_spread",
    )(parts, note)


def exact_dot(left, one_hot, contract):
    total = None
    for _ in range(3):
        part = left.astype(BF16)
        left = left - part.astype(F32)
        term = lax.dot_general(part, one_hot, contract, preferred_element_type=F32)
        total = term if total is None else total + term
    return total


def finish_kernel(
    factor, far_ref, near_ref, own_ref, scale_ref, head_ref, act_ref, parity_ref,
    own_tag_ref, near_tag_ref, far_tag_ref, out_ref, gram_ref, tag_ref,
):
    cap = own_ref.shape[0]
    gram_ref[...] = head_ref[...]
    add_grams(gram_ref, far_ref, near_ref, own_ref, scale_ref, parity_ref, slice(None))
    product = gram_ref[...] * act_ref[...].astype(F32)
    lane = lax.broadcasted_iota(jnp.int32, (cap, TAG), 1) // 32
    odd = (parity_ref[0] == 1).astype(F32)
    own, near, far = (ref[...].astype(F32) for ref in (own_tag_ref, near_tag_ref, far_tag_ref))
    last = odd * far + (1.0 - odd) * own
    left = odd * own + (1.0 - odd) * far
    tag_ref[...] = jnp.zeros_like(tag_ref)
    tag_ref[:cap] = jnp.where(lane == 1, near, 0.0).astype(BF16)
    tag_ref[cap : 2 * cap] = jnp.where(lane == 2, last, 0.0).astype(BF16)
    tag_ref[OWN : OWN + cap] = jnp.where(lane == 3, own, 0.0).astype(BF16)
    by_column = exact_dot(product, tag_ref[...], (((1,), (0,)), ((), ())))[:cap]
    by_row = (((0,), (0,)), ((), ()))
    pairs = exact_dot(by_column, left.astype(BF16), by_row)
    selves = exact_dot(by_column, own.astype(BF16), by_row)
    shape = (32, TAG)
    column = lax.broadcasted_iota(jnp.int32, shape, 0) // 4
    place = lax.broadcasted_iota(jnp.int32, shape, 1)
    out_ref[...] = factor * (
        jnp.where((place < 8) & (place != column), selves[96:128], 0.0)
        + jnp.where((place >= 8) & (place < 16), pairs[32:64], 0.0)
        + jnp.where((place >= 16) & (place < 24), pairs[64:96], 0.0)
    )


def finish(factor, own, near, far, scale, head_gram, act_gram, parity, tags):
    tag_at = tags[0].shape[1] // TAG - 1
    last = scale.shape[1] // PART - 1
    cap = own.shape[0]
    block = pl.BlockSpec((cap, PART), lambda step: (0, 0))
    whole = pl.BlockSpec((TALL, WIDE), lambda step: (0, 0))
    tag = pl.BlockSpec((cap, TAG), lambda step: (0, tag_at))
    return pl.pallas_call(
        functools.partial(finish_kernel, factor),
        grid=(1,),
        in_specs=[
            block,
            block,
            block,
            pl.BlockSpec((1, PART), lambda step: (0, last)),
            whole,
            whole,
            pl.BlockSpec(memory_space=pltpu.SMEM),
            tag,
            tag,
            tag,
        ],
        out_specs=pl.BlockSpec((32, TAG), lambda step: (0, 0)),
        out_shape=jax.ShapeDtypeStruct((32, TAG), F32),
        scratch_shapes=[pltpu.VMEM((TALL, WIDE), F32), pltpu.VMEM((WIDE, TAG), BF16)],
        compiler_params=pltpu.CompilerParams(vmem_limit_bytes=VMEM_LIMIT),
        name="finish",
    )(far, near, own, scale, head_gram, act_gram, parity, *tags)


def far_swap(value):
    count = lax.axis_size("ex")
    pairs = [(e, (e + (2 if e % 2 else -2)) % count) for e in range(count)]
    return lax.ppermute(value, "ex", pairs)


def near_swap(value):
    count = lax.axis_size("ex")
    return lax.ppermute(value, "ex", [(e, e ^ 1) for e in range(count)])


def sum_over_width(value, note):
    parts = lax.axis_size("width")
    split = value.reshape(parts, TALL // parts, WIDE)
    spread, most = sum_and_spread(lax.all_to_all(split, "width", 0, 0), note)
    return lax.all_to_all(spread, "width", 0, 0).reshape(TALL, WIDE), most


def packed(cap, activations, gradients, act_scale, grad_scale, counts, loss_mask):
    ex_local, tok_slots = loss_mask.shape
    row_count = ex_local * tok_slots
    own_acts = activations[0].reshape(row_count, -1)
    own_grads = gradients[0].reshape(row_count, -1)
    parity = (lax.axis_index("ex") % 2).astype(jnp.int32).reshape(1)
    factor = 1.0 / (math.sqrt(D * FF) * tok_slots)

    acts, pick, many = pack_acts(counts, loss_mask, own_acts, cap)
    near_acts, far_acts = near_swap(acts), far_swap(acts)
    head, tail = pack_grads(pick, own_grads, near_acts)
    far_head, far_tail = far_swap(head), far_swap(tail)
    near_head, near_tail = near_swap(head), near_swap(tail)

    many = lax.all_to_all(many, "ex", 0, 0, tiled=True)
    act_gram = gram(acts, near_acts, far_acts, act_scale, parity)
    act_gram, most = sum_over_width(act_gram, many)
    head_gram = head_grams(head, near_head, far_head, grad_scale, parity)
    scores = finish(
        factor, tail, near_tail, far_tail, grad_scale, head_gram, act_gram, parity,
        (acts, near_acts, far_acts),
    )
    mine = lax.all_to_all(scores, ("layer", "width"), 0, 0, tiled=True).sum(axis=0)
    count = lax.axis_size("ex")
    ahead = lax.ppermute(mine, "ex", [(e, (e + 2) % count) for e in range(0, count, 2)])
    place = lax.broadcasted_iota(jnp.int32, mine.shape, 0)
    kept = jnp.where((place < 8) | (parity[0] == 1), mine, ahead)
    return kept[: 8 * (HOPS + 1)].reshape(HOPS + 1, ex_local, 1), most[0, 0]


def local(activations, gradients, act_scale, grad_scale, counts, loss_mask):
    args = (activations, gradients, act_scale, grad_scale, counts, loss_mask)
    quick, most = packed(CAPS[0], *args)

    def whole():
        ex_local, tok_slots = loss_mask.shape
        positions = lax.broadcasted_iota(jnp.int32, (ex_local, tok_slots), 1)
        token_weight = (positions < counts[:, None]).astype(jnp.int32) * loss_mask
        weight_rows = token_weight.astype(F32).reshape(ex_local * tok_slots)
        return plain(activations, gradients, act_scale, grad_scale, weight_rows, tok_slots)

    def larger():
        return lax.cond(most > CAPS[1], whole, lambda: packed(CAPS[1], *args)[0])

    return lax.cond(most > CAPS[0], larger, lambda: quick)


def solution(mesh):
    in_specs = (
        P("layer", "ex", None, "width"),
        P("layer", "ex", None, "width"),
        P("layer", "width"),
        P("layer", "width"),
        P("ex"),
        P("ex", None),
    )
    out_specs = P(None, "ex", "layer")
    return jax.shard_map(local, mesh=mesh, in_specs=in_specs, out_specs=out_specs, check_vma=False)
```
